256 devices in a mesh: section: 8 (over z_lo, x), expert: 32 (over z_hi, y, core).
Axes of the slice: x: 4, y: 4, z: 8 (z_hi: 4, z_lo: 2; z = z_hi * 2 + z_lo), core: 2. Of those that a mesh axis runs over, the one named last changes fastest.
Arguments:
- queries: bfloat16 [8, 512, 36864], P('section', None, 'expert'), may hold values from -48 to 48
- stretch_latents: bfloat16 [8, 512, 576], P('section', 'expert'), may hold values from -6 to 6
- pool_latents: bfloat16 [8, 3072, 576], P('section', 'expert'), may hold values from -6 to 6
- stretch_offset: int32 [8], P('section'), may hold values from 0 to 3072
- value_up: bfloat16 [8, 64, 512, 128], P('section', 'expert'), may hold values from -0.75 to 0.75
- out_proj: bfloat16 [8, 8192, 7168], P('section', 'expert'), may hold values from -0.25 to 0.25
- resid: bfloat16 [8, 512, 7168], P('section', 'expert'), may hold values from -6 to 6
- norm_gain: float32 [8, 7168], P('section'), may hold values from 0.1 to 1.9
- expert_ids: int32 [8, 512, 2], P('section', 'expert'), may hold values from 0 to 3, all different within a row; in each aligned block of 16 rows (0 to 15, 16 to 31, ..., all dimensions but the last counted through in order) at most 12 rows name the same one
- route_weight: float32 [8, 512, 2], P('section', 'expert'), may hold values from 0.05 to 1
- gate_up: bfloat16 [8, 32, 7168, 2, 128], P('section', 'expert'), may hold values from -0.0625 to 0.0625
- down_proj: bfloat16 [8, 32, 128, 7168], P('section', 'expert'), may hold values from -0.1875 to 0.1875
- page_owner: int32 [8, 32], P('section', 'expert'), may hold values from 0 to 7
Outputs:
- layer_out: bfloat16 [8, 512, 7168], P('section', 'expert')
- page_store: bfloat16 [8, 32, 8, 9216], P('section', 'expert')
The draws below stay inside these ranges and needn't reach their ends.
Inputs may be any that keep to these rules, and one draw needn't show every extreme that they name: `expert_ids`: in the 16 tokens of one device no expert is named by more than 12 tokens.
All inputs are finite; a program needn't handle non-finite values.
Results may differ from the reference program's by a relative error of at most 0.029.
Values may be sent and summed in bfloat16 or wider, within the bound.
A program may use at most 128 MiB of HBM per device.

```python
import math
import jax
import jax.numpy as jnp
import numpy as np
from jax import lax

D = 7168
HEADS = 64
LAT = 512
ROPE = 64
LATW = 576
HEAD_DIM = 128
FF_E = 1024
EXP_SPAN = 8
HID_DEV = 128
EXPERTS = 4
TOPK = 2
STRETCH = 512
POOL = 3072
PAGE = 16
T_DEV = 16
CAP = 12
N_SECTION = 8
N_EXPERT = 32


def shared_latents(key):
    base = jnp.clip(jax.random.normal(jax.random.fold_in(key, 101), (N_SECTION, STRETCH, LATW), jnp.float32), -6.0, 6.0)
    return base


def draw_stretch_latents(key, part):
    base = shared_latents(key)
    return base.astype(jnp.bfloat16)


def draw_queries(key, part):
    key = jax.random.fold_in(key, 5)
    values = jnp.clip(jax.random.normal(key, (N_SECTION, STRETCH, HEADS * LATW), jnp.float32), -6.0, 6.0)
    return values.astype(jnp.bfloat16)


def touch_ends(values, own_key, least, high):
    longest = values.shape.index(max(values.shape))
    spots = []
    for shift in (0, 1):
        where = [jax.random.randint(jax.random.fold_in(own_key, axis), (), 0, length) for axis, length in enumerate(values.shape)]
        where[longest] = (where[longest] + shift) % values.shape[longest]
        spots.append(tuple(where))
    return values.at[spots[0]].set(least).at[spots[1]].set(high)


def shard_levels(key, dims, shards, low, high):
    def one(axis_at, shards_of):
        draws = jax.random.uniform(jax.random.fold_in(jax.random.fold_in(key, 6), axis_at), (shards_of,), jnp.float32, low / len(shards), high / len(shards))
        return jnp.repeat(jnp.exp(draws), dims[axis_at] // shards_of).reshape((-1,) + (1,) * (len(dims) - axis_at - 1))

    loudness = one(*shards[0])
    for cut in shards[1:]:
        loudness = loudness * one(*cut)
    return loudness


def assign_block(rng, own, number, rows, number_of, top, reach, slope):
    order = jax.random.permutation(rng, number_of)
    crowded, common = load_shares(number_of, rows * top, reach, slope, True), load_shares(number_of, rows * top, reach, slope, False)
    places = jnp.arange(number_of)

    def named(sizes, turn):
        used = int((sizes > 0).sum())
        fixed = max(1, used // 4)
        shifted = fixed + (places - fixed + turn * (used - fixed)) % max(1, number_of - fixed)
        return jnp.zeros((number_of,), jnp.int32).at[order[jnp.where(places < fixed, places, shifted)]].set(jnp.asarray(sizes, jnp.int32))

    sizes = jnp.where(number % 4 == 0, named(crowded, number // 4), named(common, number - number // 4 - 1))
    mixed = jax.random.permutation(jax.random.fold_in(own, 3), number_of)
    source_of, receiver = mixed[0:number_of // 2 * 2:2], mixed[1:number_of // 2 * 2:2]
    room = jnp.minimum(sizes[source_of] - 1, reach - sizes[receiver]) // 2
    room = jnp.where((source_of == order[0]) | (receiver == order[0]) | (sizes[receiver] == 0), 0, jnp.maximum(room, 0))
    shifted = jax.random.randint(jax.random.fold_in(own, 4), (number_of // 2,), 0, 1 << 20) % (room + 1)
    sizes = sizes.at[source_of].add(-shifted).at[receiver].add(shifted)
    items = jnp.searchsorted(jnp.cumsum(sizes), jnp.arange(rows * top), side="right").astype(jnp.int32)
    table = items.reshape(top, rows).T
    table = table[jax.random.permutation(jax.random.fold_in(own, 1), rows)]
    turn = jax.random.randint(jax.random.fold_in(own, 2), (rows, 1), 0, top)
    return jnp.take_along_axis(table, (jnp.arange(top)[None, :] + turn) % top, axis=1)


def load_shares(amount, total, bound, lean, full):
    loads = [(1 << 20) // math.isqrt(rank ** lean) + 1 for rank in range(1, amount + 1)]
    largest = bound if full else min(bound, max(-(-total // amount), total * loads[0] // sum(loads)))
    least = 1 if total - largest >= amount - 1 else 0
    holding, spare = [largest] + [least] * (amount - 1), total - largest - least * (amount - 1)
    while spare > 0:
        free = [i for i in range(1, amount) if holding[i] < largest] or [i for i in range(1, amount) if holding[i] < bound]
        mass, remaining = sum([loads[i] for i in free]), spare
        for i in free:
            extra = min(bound - holding[i], max(1, remaining * loads[i] // mass), spare)
            holding[i] = holding[i] + extra
            spare = spare - extra
    return np.array(holding)


def bell_draw(key, extent, scale, reach, shards=(), held_as=jnp.bfloat16):
    gain = shard_levels(key, extent, shards, -0.22, 0.18) if shards else 1.0
    drawn = jax.random.normal(key, extent, jnp.float32) * scale * gain
    return jnp.minimum(jnp.maximum(drawn, -reach), reach).astype(held_as)


def setup_inputs(seed: int = 0) -> dict:
    arg_keys = jax.random.split(jax.random.key(seed), 14)
    queries = draw_queries(jax.random.fold_in(arg_keys[13], 71), 0)
    stretch_latents = draw_stretch_latents(jax.random.fold_in(arg_keys[13], 71), 0)
    pool_latents = bell_draw(arg_keys[2], (N_SECTION, POOL, LATW), 1.0, 6.0, ((0, 8), (1, 32)))
    stretch_offset = touch_ends(jax.random.randint(arg_keys[3], (N_SECTION,), 0, POOL + 1), jax.random.fold_in(arg_keys[3], 1), 0, POOL).astype(jnp.int32)
    value_up = bell_draw(arg_keys[4], (N_SECTION, HEADS, LAT, HEAD_DIM), (LAT // 8) ** -0.5, 0.75, ((0, 8), (1, 32)))
    out_proj = bell_draw(arg_keys[5], (N_SECTION, HEADS * HEAD_DIM, D), (HEADS * HEAD_DIM // 16) ** -0.5, 0.25, ((0, 8), (1, 32)))
    resid = bell_draw(arg_keys[6], (N_SECTION, STRETCH, D), 1.0, 6.0, ((0, 8), (1, 32)))
    norm_gain = jnp.clip(1.0 + 0.18 * jax.random.normal(arg_keys[7], (N_SECTION, D), jnp.float32), 0.1, 1.9)
    expert_ids_keys = jax.random.split(jax.random.fold_in(arg_keys[8], 1), N_SECTION * STRETCH // T_DEV)
    expert_ids_turns = jax.random.permutation(jax.random.fold_in(arg_keys[8], 3), N_SECTION * STRETCH // T_DEV)
    expert_ids = jax.vmap(lambda own, number: assign_block(jax.random.fold_in(arg_keys[8], 2), own, number, T_DEV, EXPERTS, TOPK, CAP, 2))(expert_ids_keys, expert_ids_turns).reshape((N_SECTION, STRETCH, TOPK))
    route_weight = jnp.clip(jnp.exp(math.log(1.0) - 2.9957323 * jax.random.uniform(arg_keys[9], (N_SECTION, STRETCH, TOPK), jnp.float32) ** shard_levels(arg_keys[9], (N_SECTION, STRETCH, TOPK), ((0, 8), (1, 32)), -0.2, 0.2)), 0.05, 1.0)
    gate_up = bell_draw(arg_keys[10], (N_SECTION, N_EXPERT, D, 2, HID_DEV), D ** -0.5, 0.0625, ((0, 8), (1, 32)))
    down_proj = bell_draw(arg_keys[11], (N_SECTION, N_EXPERT, HID_DEV, D), FF_E ** -0.5, 0.1875, ((0, 8), (1, 32)))
    page_owner = touch_ends(jax.random.randint(arg_keys[12], (N_SECTION, STRETCH // PAGE), 0, N_SECTION), jax.random.fold_in(arg_keys[12], 1), 0, N_SECTION - 1).astype(jnp.int32)
    return dict(queries=queries, stretch_latents=stretch_latents, pool_latents=pool_latents, stretch_offset=stretch_offset, value_up=value_up, out_proj=out_proj, resid=resid, norm_gain=norm_gain, expert_ids=expert_ids, route_weight=route_weight, gate_up=gate_up, down_proj=down_proj, page_owner=page_owner)


def attend(query, keys, offset):
    position = jnp.arange(POOL + STRETCH, dtype=jnp.int32)
    token = jnp.arange(STRETCH, dtype=jnp.int32)
    visible = jnp.where((position < POOL)[None, :], (position < offset)[None, :], (position - POOL)[None, :] <= token[:, None])
    scores = jnp.dot(query, keys.T, preferred_element_type=jnp.float32) * (1.0 / math.sqrt(HEAD_DIM + ROPE))
    top = lax.optimization_barrier(jnp.max(jnp.where(visible, scores, -1e+30), axis=1, keepdims=True))
    probs = jnp.where(visible, jnp.exp(scores - top), 0.0)
    denom = lax.optimization_barrier(jnp.sum(probs, axis=1, keepdims=True))
    mixed = jnp.dot(probs.astype(jnp.bfloat16), keys[:, :LAT], preferred_element_type=jnp.float32) / denom
    return mixed.astype(jnp.bfloat16)

def reference(queries, stretch_latents, pool_latents, stretch_offset, value_up, out_proj, resid, norm_gain, expert_ids, route_weight, gate_up, down_proj, page_owner):
    groups = HEADS // N_EXPERT
    outputs = []
    pages_all = []
    for section_idx in range(N_SECTION):
        keys = jnp.concatenate([pool_latents[section_idx], stretch_latents[section_idx]], axis=0)
        query = queries[section_idx].reshape(STRETCH, HEADS, LATW)
        offset = stretch_offset[section_idx]

        def head(h):
            latent = attend(query[:, h, :], keys, offset)
            return jnp.dot(latent, value_up[section_idx, h], preferred_element_type=jnp.float32).astype(jnp.bfloat16)
        heads_out = lax.map(head, jnp.arange(HEADS, dtype=jnp.int32))
        grouped = heads_out.reshape(N_EXPERT, groups, STRETCH, HEAD_DIM)
        weights_out = out_proj[section_idx].reshape(N_EXPERT, groups * HEAD_DIM, D)

        def add_group(total, pair):
            block, weight = pair
            rows = block.transpose(1, 0, 2).reshape(STRETCH, groups * HEAD_DIM)
            term = jnp.dot(rows, weight, preferred_element_type=jnp.float32).astype(jnp.bfloat16).astype(jnp.float32)
            return (total + term, None)
        attn, _ = lax.scan(add_group, jnp.zeros((STRETCH, D), jnp.float32), (grouped, weights_out))
        mid = resid[section_idx].astype(jnp.float32) + attn
        normed = (mid * lax.rsqrt(lax.optimization_barrier(jnp.mean(mid * mid, axis=-1, keepdims=True)) + 1e-06) * norm_gain[section_idx]).astype(jnp.bfloat16)
        scores_r = route_weight[section_idx]
        share = (2.827 * scores_r / lax.optimization_barrier(jnp.sum(scores_r, axis=-1, keepdims=True))).astype(jnp.bfloat16)
        chosen = (expert_ids[section_idx][:, :, None] == jnp.arange(EXPERTS, dtype=jnp.int32)).astype(jnp.float32)
        table = lax.optimization_barrier(jnp.sum(chosen * share.astype(jnp.float32)[:, :, None], axis=1))

        def add_slice(total, j):
            expert = j // EXP_SPAN
            weight_in = gate_up[section_idx, j].reshape(D, 2 * HID_DEV)
            both = jnp.dot(normed, weight_in, preferred_element_type=jnp.float32)
            gate = both[:, :HID_DEV]
            upper = both[:, HID_DEV:]
            factor = lax.optimization_barrier(jnp.sum(table * (jnp.arange(EXPERTS, dtype=jnp.int32) == expert), axis=1))
            hidden = (factor[:, None] * (jax.nn.silu(gate) * upper)).astype(jnp.bfloat16)
            part = jnp.dot(hidden, down_proj[section_idx, j], preferred_element_type=jnp.float32).astype(jnp.bfloat16).astype(jnp.float32)
            return (total + part, None)
        moe, _ = lax.scan(add_slice, jnp.zeros((STRETCH, D), jnp.float32), jnp.arange(N_EXPERT, dtype=jnp.int32))
        outputs.append((mid + moe).astype(jnp.bfloat16))
        pages_all.append(stretch_latents[section_idx].reshape(STRETCH // PAGE, PAGE * LATW))
    layer_out = jnp.stack(outputs, axis=0)
    pages = jnp.stack(pages_all, axis=0).transpose(1, 0, 2)
    owners = page_owner.T
    match = owners[None, :, :] == jnp.arange(N_SECTION, dtype=jnp.int32)[:, None, None]
    page_store = jnp.where(match[:, :, :, None], pages[None], jnp.zeros((), jnp.bfloat16)).astype(jnp.bfloat16)
    return (layer_out, page_store)
```

```python
import math

import jax
import jax.numpy as jnp
from jax import lax
from jax.experimental import pallas as pl
from jax.experimental.pallas import tpu as pltpu
from jax.sharding import PartitionSpec as P

MESH = pl.DeviceIdType.MESH
BF = jnp.bfloat16
F32 = jnp.float32
D = 7168
HALF = D // 2
QUART = D // 4
LAT = 512
LATW = 576
WIDE = 640
HEAD_DIM = 128
POOL_DEV = 96
TOK = 16
BLK = POOL_DEV + TOK
STRETCH = 512
CAP = 12
SLOTS = 2 * CAP
ROWS = 2 * SLOTS
TILE = 256
GROUP = 4 * 2 * BLK
NSEC = 8
NEG = -1e30
SCORE = math.log2(math.e) / math.sqrt(192.0)

N_KEY = 31
N_MOE = 32


def one_hot(mask):
    return jnp.where(mask, 1.0, 0.0).astype(BF)


def kernel(
    offset_ref, owner_ref, query_ref, stretch_ref, pool_ref, vup_ref, wo_ref, resid_ref, gain_ref,
    ids_ref, rw_ref, gu_ref, wd_ref,
    out_ref, pages_ref,
    q_raw, qs, keys, acc, ms, ls, ho, wo, wd, gu_raw, w_in, vup, res, gain,
    page_out, part, r_opp, r_rel, r_pure, z_out, z_opp, z_rel, z_pure,
    mid, normed, ss, d_top, d_bot, disp, relay, got, hid,
    dpart, e_opp, e_rel, e_pure, e_out, e_relay, e_got, o_stage,
    load_sem, key_s, key_r, key_x, w_s, w_r, ho_s, ho_r, page_s, page_r,
    ry_s, ry_r, rz_s, rz_r, ss_s, ss_r, moe_s, moe_r, moe_x, rel_r, hid_s, hid_r,
    ey_s, ey_r, ez_s, ez_r, o_s, o_r,
):
    sec = lax.axis_index("section")
    me = lax.axis_index("expert")
    z = me // 8
    y = (me // 2) % 4
    c = me % 2
    d = 1 - 2 * c
    yp, ym, yo = (y + d + 4) % 4, (y - d + 4) % 4, (y + 2) % 4
    zp, zm, zo = (z + d + 4) % 4, (z - d + 4) % 4, (z + 2) % 4

    def dev(zz, yy, cc):
        return (sec, (zz * 4 + yy) * 2 + cc)

    y_plus, y_minus = dev(z, yp, c), dev(z, ym, c)
    z_plus, z_minus = dev(zp, y, c), dev(zm, y, c)
    twin = dev(z, y, 1 - c)
    barrier = pltpu.get_barrier_semaphore()
    for to in (y_plus, y_minus, z_plus, z_minus, twin):
        pl.semaphore_signal(barrier, inc=1, device_id=to, device_id_type=MESH)
    for k in range(1, NSEC):
        pl.semaphore_signal(barrier, inc=1, device_id=((sec + k) % NSEC, me), device_id_type=MESH)

    def remote(src, dst, s_sem, r_sem, to):
        return pltpu.make_async_remote_copy(
            src_ref=src, dst_ref=dst, send_sem=s_sem, recv_sem=r_sem, device_id=to, device_id_type=MESH
        )

    sent = []

    def send(src, dst, s_sem, r_sem, to):
        copy = remote(src, dst, s_sem, r_sem, to)
        copy.start()
        sent.append(copy)

    def arrived(dst, r_sem):
        remote(dst, dst, r_sem, r_sem, twin).wait_recv()

    half_c = pl.ds(pl.multiple_of(c * HALF, 128), HALF)
    half_x = pl.ds(pl.multiple_of((1 - c) * HALF, 128), HALF)

    loads = [
        pltpu.make_async_copy(query_ref, q_raw, load_sem.at[0]),
        pltpu.make_async_copy(vup_ref, vup, load_sem.at[1]),
        pltpu.make_async_copy(wo_ref.at[:, half_c], wo.at[c], load_sem.at[2]),
        pltpu.make_async_copy(gu_ref, gu_raw, load_sem.at[3]),
        pltpu.make_async_copy(wd_ref.at[:, half_c], wd.at[c], load_sem.at[4]),
        pltpu.make_async_copy(resid_ref.at[:, half_c], res.at[c], load_sem.at[5]),
        pltpu.make_async_copy(gain_ref.at[:, half_c], gain, load_sem.at[6]),
    ]
    for load in loads:
        load.start()

    lane16 = lax.broadcasted_iota(jnp.int32, (16, 128), 1)
    sub16 = lax.broadcasted_iota(jnp.int32, (16, 128), 0)
    weights = rw_ref[...]
    total = weights[0:1] + weights[1:2]
    share0 = (2.827 * weights[0:1] / total).astype(BF).astype(F32)
    share1 = (2.827 * weights[1:2] / total).astype(BF).astype(F32)
    ids = ids_ref[...]
    which = lax.broadcasted_iota(jnp.int32, (16, TOK), 0)
    table = jnp.where(ids[0:1] == which, share0, 0.0) + jnp.where(ids[1:2] == which, share1, 0.0)
    place = one_hot(lane16 == sub16 + 64 + 16 * c)
    tab = jnp.dot(table.astype(BF), place, preferred_element_type=F32).astype(BF)
    mine = pl.ds(pl.multiple_of(c * BLK, 16), BLK)
    first = pl.ds(pl.multiple_of(c * BLK, 16), POOL_DEV)
    last = pl.ds(pl.multiple_of(c * BLK + POOL_DEV, 16), TOK)
    keys[z, y, first, 512:WIDE] = jnp.zeros((POOL_DEV, 128), BF)
    keys[z, y, last, 512:WIDE] = tab
    keys[z, y, first, 0:LATW] = pool_ref[...]
    keys[z, y, last, 0:LATW] = stretch_ref[...]
    latents = stretch_ref[...]
    for g in range(NSEC):
        page_out[g] = jnp.where(owner_ref[0] == g, latents, jnp.zeros_like(latents))

    pl.semaphore_wait(barrier, 5 + NSEC - 1)

    def block(zz, yy):
        return keys.at[zz, yy, mine]

    def key_send(zz, yy, number, to):
        remote(block(zz, yy), block(zz, yy), key_s.at[number], key_r.at[zz, yy], to).start()

    def key_twin(zz, yy, number):
        remote(block(zz, yy), block(zz, yy), key_s.at[number], key_x.at[zz, yy], twin).start()

    def key_wait(zz, yy):
        arrived(block(zz, yy), key_r.at[zz, yy])

    def key_twin_wait(zz, yy):
        theirs = keys.at[zz, yy, pl.ds(pl.multiple_of((1 - c) * BLK, 16), BLK)]
        arrived(theirs, key_x.at[zz, yy])

    key_send(z, y, 0, y_plus)
    key_send(z, y, 1, y_minus)
    key_send(z, y, 2, z_plus)
    key_send(z, y, 3, z_minus)
    key_twin(z, y, 4)
    send(wo_ref.at[:, half_x], wo.at[c], w_s.at[0], w_r.at[0], twin)
    send(wd_ref.at[:, half_x], wd.at[c], w_s.at[1], w_r.at[1], twin)
    send(resid_ref.at[:, half_x], res.at[c], w_s.at[2], w_r.at[2], twin)
    for k in range(1, NSEC):
        g = (sec + k) % NSEC
        send(page_out.at[g], pages_ref.at[sec], page_s.at[k - 1], page_r.at[k - 1], (g, me))
    pages_ref[sec] = page_out[sec]

    loads[0].wait()
    lane = lax.broadcasted_iota(jnp.int32, (STRETCH, WIDE), 1)
    qs[0:STRETCH] = jnp.where(lane < LATW, q_raw[:, 0:WIDE], jnp.zeros((), BF))
    row_i = lax.broadcasted_iota(jnp.int32, (WIDE, WIDE), 0)
    col_i = lax.broadcasted_iota(jnp.int32, (WIDE, WIDE), 1)
    shift = one_hot((row_i == col_i + 64) & (col_i < LATW))
    qs[STRETCH:] = jnp.dot(q_raw[:, 512:1152], shift, preferred_element_type=F32).astype(BF)
    acc[...] = jnp.zeros_like(acc)
    ls[...] = jnp.zeros_like(ls)
    ms[...] = jnp.full(ms.shape, NEG, F32)

    def own_column(zz, number):
        key_send(zz, y, number, y_plus)
        key_send(zz, y, number + 1, y_minus)
        key_twin(zz, y, number + 2)

    key_wait(zm, y)
    key_send(zm, y, 5, z_plus)
    own_column(zm, 6)
    key_wait(zp, y)
    own_column(zp, 9)
    key_wait(zo, y)
    own_column(zo, 12)

    offset = offset_ref[0]

    def attend(yy, before):
        r = lax.broadcasted_iota(jnp.int32, (1, GROUP), 1)
        zz = (r >= 2 * BLK).astype(jnp.int32) + (r >= 4 * BLK).astype(jnp.int32) + (r >= 6 * BLK).astype(jnp.int32)
        r = r - zz * (2 * BLK)
        cc = (r >= BLK).astype(jnp.int32)
        r = r - cc * BLK
        owner = zz * 8 + yy * 2 + cc
        seen = jnp.where(owner * POOL_DEV + r < offset, -1, 1 << 20)
        limit = jnp.where(r < POOL_DEV, seen, owner * TOK + r - POOL_DEV)

        def tile(t, carry):
            before(t)
            rows = pl.ds(pl.multiple_of(t * TILE, TILE), TILE)
            part_keys = keys[:, yy].reshape(GROUP, WIDE)
            s = lax.dot_general(qs[rows], part_keys, (((1,), (1,)), ((), ())), preferred_element_type=F32)
            token = (t % 2) * TILE + lax.broadcasted_iota(jnp.int32, (TILE, 1), 0)
            s = jnp.where(limit <= token, s * SCORE, NEG)
            old = ms[rows]
            new = jnp.maximum(old, jnp.max(s, axis=1, keepdims=True))
            p = jnp.exp2(s - new[:, 0:1])
            alpha = jnp.exp2(old - new)
            ms[rows] = new
            ls[rows] = ls[rows] * alpha + jnp.sum(p, axis=1, keepdims=True)
            add = jnp.dot(p.astype(BF), part_keys[:, 0:LAT], preferred_element_type=F32)
            acc[rows] = acc[rows] * alpha[:, 0:1] + add
            return carry

        lax.fori_loop(0, 4, tile, 0)

    def near(t):
        zz = (z - d * t + 8) % 4
        key_wait(zz, ym)
        key_send(zz, ym, 15 + t, y_plus)
        key_twin(zz, ym, 19 + t)
        key_wait(zz, yp)
        key_twin(zz, yp, 23 + t)

    def far(t):
        zz = (z - d * t + 8) % 4
        key_wait(zz, yo)
        key_twin(zz, yo, 27 + t)

    def nothing(t):
        pass

    for zz in (z, zm, zp, zo):
        key_twin_wait(zz, y)
    attend(y, near)
    for zz in (z, zm, zp, zo):
        key_twin_wait(zz, ym)
    attend(ym, far)
    for zz in (z, zm, zp, zo):
        key_twin_wait(zz, yp)
    attend(yp, nothing)
    for zz in (z, zm, zp, zo):
        key_twin_wait(zz, yo)
    attend(yo, nothing)

    loads[1].wait()
    for t in range(4):
        rows = pl.ds(t * TILE, TILE)
        latent = (acc[rows] / ls[rows][:, 0:1]).astype(BF)
        head = jnp.dot(latent, vup[t // 2], preferred_element_type=F32).astype(BF)
        at = (t // 2) * HEAD_DIM
        zs = (t % 2) * 2
        ho[c, zs : zs + 2, :, :, at : at + HEAD_DIM] = head.reshape(2, 4, 32, HEAD_DIM)
    send(ho.at[c], ho.at[c], ho_s.at[0], ho_r.at[0], twin)

    loads[2].wait()
    arrived(wo.at[1 - c], w_r.at[0])
    arrived(ho.at[1 - c], ho_r.at[0])

    def project(yy):
        left = ho[0, :, yy].reshape(128, 2 * HEAD_DIM)
        right = ho[1, :, yy].reshape(128, 2 * HEAD_DIM)

        def column(n, carry):
            cols = pl.ds(pl.multiple_of(n * 896, 128), 896)
            out = jnp.dot(left, wo[0, :, cols], preferred_element_type=F32)
            out = out + jnp.dot(right, wo[1, :, cols], preferred_element_type=F32)
            part[yy, :, :, cols] = out.astype(BF).reshape(4, 32, 896)
            return carry

        lax.fori_loop(0, 4, column, 0)

    order = (zo, zm, zp, z)
    project(yo)
    for k, zz in enumerate(order):
        send(part.at[yo, zz], r_opp.at[k], ry_s.at[k], ry_r.at[k], y_plus)
    project(ym)
    for k, zz in enumerate(order):
        send(part.at[ym, zz], r_pure.at[k], ry_s.at[4 + k], ry_r.at[4 + k], y_minus)
    project(yp)
    project(y)

    loads[3].wait()
    row_p = lax.broadcasted_iota(jnp.int32, (256, 256), 0)
    col_p = lax.broadcasted_iota(jnp.int32, (256, 256), 1)
    perm = one_hot(jnp.where(row_p < 128, 2 * row_p, 2 * row_p - 255) == col_p)

    def split(i, carry):
        both = gu_raw[pl.ds(pl.multiple_of(i * 256, 256), 256)]
        out = jnp.dot(perm, both, preferred_element_type=F32).astype(BF)
        rows = pl.ds(pl.multiple_of(i * 128, 128), 128)
        w_in[rows, 0:128] = out[0:128]
        w_in[rows, 128:256] = out[128:256]
        return carry

    lax.fori_loop(0, D // 128, split, 0)

    lane_r = lax.broadcasted_iota(jnp.int32, (128, 128), 0)
    lane_c = lax.broadcasted_iota(jnp.int32, (128, 128), 1)
    same = (lane_r >= 16) == (lane_c >= 16)
    earlier = one_hot((lane_r < lane_c) & same & (lane_c < 32) & (lane_r < 32))

    def routes(zz, yy):
        both = (
            keys[zz, yy, POOL_DEV:BLK, 512:WIDE].astype(F32)
            + keys[zz, yy, BLK + POOL_DEV : 2 * BLK, 512:WIDE].astype(F32)
        )
        shares = jnp.where(lane16 < 32, pltpu.roll(both, 64, 1), 0.0)
        chosen = shares > 0.0
        rank = jnp.dot(one_hot(chosen), earlier, preferred_element_type=F32)
        slot = jnp.where(chosen, rank + jnp.where(lane16 >= 16, float(CAP), 0.0), -1.0)
        return shares, slot

    row48 = lax.broadcasted_iota(jnp.int32, (ROWS, 128), 0)
    slot48 = jnp.where(row48 >= SLOTS, row48 - SLOTS, row48).astype(F32)
    _, own_slot = routes(z, y)
    for e in range(4):
        hit = own_slot[e : e + 1] == slot48
        d_top[e * ROWS : (e + 1) * ROWS] = one_hot(hit & (row48 < SLOTS))
        d_bot[e * ROWS : (e + 1) * ROWS] = one_hot(hit & (row48 >= SLOTS))

    for k, zz in enumerate(order):
        arrived(r_opp.at[k], ry_r.at[k])
        part[yp, zz] = (part[yp, zz].astype(F32) + r_opp[k].astype(F32)).astype(BF)
        send(part.at[yp, zz], r_rel.at[k], ry_s.at[8 + k], ry_r.at[8 + k], y_plus)

    def column_sum(k):
        arrived(r_pure.at[k], ry_r.at[4 + k])
        arrived(r_rel.at[k], ry_r.at[8 + k])
        return part[y, order[k]].astype(F32) + r_rel[k].astype(F32) + r_pure[k].astype(F32)

    z_out[0] = column_sum(0).astype(BF)
    send(z_out.at[0], z_opp, rz_s.at[0], rz_r.at[0], z_plus)
    z_out[1] = column_sum(1).astype(BF)
    send(z_out.at[1], z_pure, rz_s.at[1], rz_r.at[1], z_minus)
    ahead = column_sum(2)
    arrived(z_opp, rz_r.at[0])
    z_out[2] = (ahead + z_opp[...].astype(F32)).astype(BF)
    send(z_out.at[2], z_rel, rz_s.at[2], rz_r.at[2], z_plus)
    mid[...] = column_sum(3)

    loads[5].wait()
    loads[6].wait()
    arrived(res.at[1 - c], w_r.at[2])
    arrived(z_pure, rz_r.at[1])
    arrived(z_rel, rz_r.at[2])
    middle = mid[...] + z_pure[...].astype(F32) + z_rel[...].astype(F32)
    middle = middle + res[...].reshape(32, HALF).astype(F32)
    mid[...] = middle
    ss[0] = jnp.broadcast_to(jnp.sum(middle * middle, axis=1, keepdims=True), (32, 128))
    send(ss.at[0], ss.at[1], ss_s.at[0], ss_r.at[0], twin)
    arrived(ss.at[1], ss_r.at[0])
    scale = lax.rsqrt((ss[0] + ss[1])[:, 0:1] * (1.0 / D) + 1e-06)
    normed[...] = (mid[...] * scale * gain[...]).astype(BF)

    for n in range(2):
        lo = n * 896
        out = jnp.dot(d_top[:, 0:32], normed[:, lo : lo + 896], preferred_element_type=F32)
        out = out + jnp.dot(d_bot[:, 0:32], normed[:, QUART + lo : QUART + lo + 896], preferred_element_type=F32)
        disp[:, :, lo : lo + 896] = out.astype(BF).reshape(4, ROWS, 896)

    def slab(zz, yy):
        return got.at[c, zz, yy]

    def moe_send(zz, yy, number, to):
        remote(slab(zz, yy), slab(zz, yy), moe_s.at[number], moe_r.at[zz, yy], to).start()

    def moe_twin(zz, yy, number):
        remote(slab(zz, yy), slab(zz, yy), moe_s.at[number], moe_x.at[zz, yy], twin).start()

    def moe_wait(zz, yy):
        arrived(slab(zz, yy), moe_r.at[zz, yy])

    def moe_column(zz, number):
        moe_send(zz, y, number, y_plus)
        moe_send(zz, y, number + 1, y_minus)
        moe_twin(zz, y, number + 2)

    remote(disp.at[zo], relay, moe_s.at[0], rel_r.at[0], z_plus).start()
    remote(disp.at[zp], slab(z, y), moe_s.at[1], moe_r.at[z, y], z_plus).start()
    remote(disp.at[zm], slab(z, y), moe_s.at[2], moe_r.at[z, y], z_minus).start()
    got[c, z, y] = disp[z]
    moe_column(z, 4)
    arrived(relay, rel_r.at[0])
    remote(relay, slab(zm, y), moe_s.at[3], moe_r.at[zm, y], z_plus).start()
    moe_wait(zm, y)
    moe_column(zm, 7)
    moe_wait(zp, y)
    moe_column(zp, 10)
    moe_wait(zo, y)
    moe_column(zo, 13)

    def moe_near(t, carry):
        zz = (z - d * t + 8) % 4
        moe_wait(zz, ym)
        moe_send(zz, ym, 16 + t, y_plus)
        moe_twin(zz, ym, 20 + t)
        moe_wait(zz, yp)
        moe_twin(zz, yp, 24 + t)
        return carry

    def moe_far(t, carry):
        zz = (z - d * t + 8) % 4
        moe_wait(zz, yo)
        moe_twin(zz, yo, 28 + t)
        return carry

    slot24 = lax.broadcasted_iota(jnp.int32, (SLOTS, 128), 0).astype(F32)

    def experts(yy, number):
        for zz in (z, zm, zp, zo):
            arrived(got.at[1 - c, zz, yy], moe_x.at[zz, yy])
        top = jnp.zeros((4 * ROWS, 256), F32)
        bottom = jnp.zeros((4 * ROWS, 256), F32)
        for k in range(2):
            rows = got[k, :, yy].reshape(4 * ROWS, QUART)
            at = 2 * k * QUART
            top = top + jnp.dot(rows, w_in[at : at + QUART], preferred_element_type=F32)
            bottom = bottom + jnp.dot(rows, w_in[at + QUART : at + 2 * QUART], preferred_element_type=F32)
        for zz in range(4):
            at = zz * ROWS
            both = top[at : at + SLOTS] + bottom[at + SLOTS : at + ROWS]
            gate, upper = both[:, 0:128], both[:, 128:256]
            shares, slot = routes(zz, yy)
            mine_e = sub16 == z
            share = jnp.sum(jnp.where(mine_e, shares, 0.0), axis=0, keepdims=True)
            place_e = jnp.sum(jnp.where(mine_e, slot, 0.0), axis=0, keepdims=True)
            factor = jnp.sum(jnp.where(place_e == slot24, share, 0.0), axis=1, keepdims=True)
            hidden = factor * (gate * (1.0 / (1.0 + jnp.exp(-gate))) * upper)
            hid[c, yy, at : at + ROWS] = jnp.concatenate([hidden, hidden], axis=0).astype(BF)
        send(hid.at[c, yy], hid.at[c, yy], hid_s.at[number], hid_r.at[yy], twin)

    upper_half = (lax.broadcasted_iota(jnp.int32, (4, ROWS, 1), 1) < SLOTS).reshape(4 * ROWS, 1)

    def down(yy):
        arrived(hid.at[1 - c, yy], hid_r.at[yy])
        left, right = hid[0, yy], hid[1, yy]

        def column(n, carry):
            lo = pl.ds(pl.multiple_of(n * 256, 128), 256)
            hi = pl.ds(pl.multiple_of(QUART + n * 256, 128), 256)
            a = jnp.dot(left, wd[0, :, lo], preferred_element_type=F32)
            a = a + jnp.dot(right, wd[1, :, lo], preferred_element_type=F32)
            b = jnp.dot(left, wd[0, :, hi], preferred_element_type=F32)
            b = b + jnp.dot(right, wd[1, :, hi], preferred_element_type=F32)
            dpart[yy, :, :, lo] = jnp.where(upper_half, a, b).astype(BF).reshape(4, ROWS, 256)
            return carry

        lax.fori_loop(0, QUART // 256, column, 0)

    loads[4].wait()
    arrived(wd.at[1 - c], w_r.at[1])
    lax.fori_loop(0, 4, moe_near, 0)
    experts(y, 0)
    experts(ym, 1)
    experts(yp, 2)
    lax.fori_loop(0, 4, moe_far, 0)
    down(ym)
    for k, zz in enumerate(order):
        send(dpart.at[ym, zz], e_pure.at[k], ey_s.at[4 + k], ey_r.at[4 + k], y_minus)
    experts(yo, 3)
    down(yo)
    for k, zz in enumerate(order):
        send(dpart.at[yo, zz], e_opp.at[k], ey_s.at[k], ey_r.at[k], y_plus)
    down(yp)
    down(y)
    for k, zz in enumerate(order):
        arrived(e_opp.at[k], ey_r.at[k])
        dpart[yp, zz] = (dpart[yp, zz].astype(F32) + e_opp[k].astype(F32)).astype(BF)
        send(dpart.at[yp, zz], e_rel.at[k], ey_s.at[8 + k], ey_r.at[8 + k], y_plus)

    def plane_sum(k):
        arrived(e_pure.at[k], ey_r.at[4 + k])
        arrived(e_rel.at[k], ey_r.at[8 + k])
        s = dpart[y, order[k]].astype(F32) + e_rel[k].astype(F32) + e_pure[k].astype(F32)
        return s.astype(BF)

    e_out[0] = plane_sum(0)
    send(e_out.at[0], e_relay, ez_s.at[0], ez_r.at[0], z_plus)
    e_out[1] = plane_sum(1)
    send(e_out.at[1], e_got.at[z], ez_s.at[1], ez_r.at[1 + z], z_minus)
    e_out[2] = plane_sum(2)
    send(e_out.at[2], e_got.at[z], ez_s.at[2], ez_r.at[1 + z], z_plus)
    arrived(e_relay, ez_r.at[0])
    send(e_relay, e_got.at[zm], ez_s.at[3], ez_r.at[1 + zm], z_plus)
    e_got[z] = plane_sum(3)
    for zz in (zm, zp, zo):
        arrived(e_got.at[zz], ez_r.at[1 + zz])
    for n in range(2):
        rows = e_got[:, :, n * 896 : (n + 1) * 896].reshape(4 * ROWS, 896)
        for h, pick in enumerate((d_top, d_bot)):
            at = h * QUART + n * 896
            moe = lax.dot_general(pick[:, 0:32], rows, (((0,), (0,)), ((), ())), preferred_element_type=F32)
            o_stage[:, :, at : at + 896] = (mid[:, at : at + 896] + moe).astype(BF).reshape(2, TOK, 896)
    send(o_stage.at[1 - c], out_ref.at[:, half_c], o_s.at[0], o_r.at[0], twin)
    out_ref[:, half_c] = o_stage[c]
    arrived(out_ref.at[:, half_x], o_r.at[0])

    for k in range(1, NSEC):
        g = (sec - k + NSEC) % NSEC
        arrived(pages_ref.at[g], page_r.at[k - 1])
    for copy in sent:
        copy.wait_send()

    def key_done(i, carry):
        remote(block(z, y), block(z, y), key_s.at[i], key_r.at[z, y], twin).wait_send()
        return carry

    lax.fori_loop(0, N_KEY, key_done, 0)

    def moe_done(i, carry):
        remote(slab(z, y), slab(z, y), moe_s.at[i], moe_r.at[z, y], twin).wait_send()
        return carry

    lax.fori_loop(0, N_MOE, moe_done, 0)


def body(
    queries, stretch_latents, pool_latents, stretch_offset, value_up, out_proj, resid, norm_gain,
    expert_ids, route_weight, gate_up, down_proj, page_owner,
):
    anywhere = pl.BlockSpec(memory_space=pl.ANY)
    vmem = pl.BlockSpec(memory_space=pltpu.VMEM)
    smem = pl.BlockSpec(memory_space=pltpu.SMEM)
    V = pltpu.VMEM
    S = lambda *shape: pltpu.SemaphoreType.DMA(shape)
    scratch = [
        V((STRETCH, 2 * LATW), BF), V((2 * STRETCH, WIDE), BF), V((4, 4, 2 * BLK, WIDE), BF),
        V((2 * STRETCH, LAT), F32), V((2 * STRETCH, 128), F32), V((2 * STRETCH, 128), F32),
        V((2, 4, 4, 32, 256), BF), V((2, 256, HALF), BF), V((2, 128, HALF), BF),
        V((2 * D, 128), BF), V((D, 256), BF), V((2, LAT, HEAD_DIM), BF),
        V((2, TOK, HALF), BF), V((1, HALF), F32),
        V((NSEC, TOK, LATW), BF), V((4, 4, 32, HALF), BF),
        V((4, 32, HALF), BF), V((4, 32, HALF), BF), V((4, 32, HALF), BF),
        V((3, 32, HALF), BF), V((32, HALF), BF), V((32, HALF), BF), V((32, HALF), BF),
        V((32, HALF), F32), V((32, HALF), BF), V((2, 32, 128), F32),
        V((4 * ROWS, 128), BF), V((4 * ROWS, 128), BF),
        V((4, ROWS, QUART), BF), V((ROWS, QUART), BF), V((2, 4, 4, ROWS, QUART), BF),
        V((2, 4, 4 * ROWS, 128), BF),
        V((4, 4, ROWS, QUART), BF),
        V((4, ROWS, QUART), BF), V((4, ROWS, QUART), BF), V((4, ROWS, QUART), BF),
        V((3, ROWS, QUART), BF), V((ROWS, QUART), BF), V((4, ROWS, QUART), BF),
        V((2, TOK, HALF), BF),
        S(7), S(N_KEY), S(4, 4), S(4, 4), S(3), S(3), S(1), S(1), S(7), S(7),
        S(12), S(12), S(3), S(3), S(1), S(1), S(N_MOE), S(4, 4), S(4, 4), S(1), S(4), S(4),
        S(12), S(12), S(4), S(5), S(1), S(1),
    ]
    out, pages = pl.pallas_call(
        kernel,
        out_shape=(
            jax.ShapeDtypeStruct((TOK, D), BF),
            jax.ShapeDtypeStruct((NSEC, TOK, LATW), BF),
        ),
        in_specs=[smem, smem, anywhere, vmem, vmem, anywhere, anywhere, anywhere, anywhere, vmem, vmem, anywhere, anywhere],
        out_specs=(vmem, vmem),
        scratch_shapes=scratch,
        compiler_params=pltpu.CompilerParams(
            collective_id=0, has_side_effects=True, vmem_limit_bytes=60 * 1024 * 1024
        ),
    )(
        stretch_offset,
        page_owner[0],
        queries[0],
        stretch_latents[0],
        pool_latents[0],
        value_up[0],
        out_proj[0],
        resid[0],
        norm_gain,
        expert_ids[0].T,
        route_weight[0].T,
        gate_up[0, 0].reshape(2 * D, 128),
        down_proj[0, 0],
    )
    return out[None], pages.reshape(1, 1, NSEC, TOK * LATW)


def solution(mesh):
    placed = (
        P("section", None, "expert"),
        P("section", "expert", None),
        P("section", "expert", None),
        P("section"),
        P("section", "expert", None, None),
        P("section", "expert", None),
        P("section", "expert", None),
        P("section", None),
        P("section", "expert", None),
        P("section", "expert", None),
        P("section", "expert", None, None, None),
        P("section", "expert", None, None),
        P("section", "expert"),
    )
    return jax.shard_map(
        body,
        mesh=mesh,
        in_specs=placed,
        out_specs=(P("section", "expert", None), P("section", "expert", None, None)),
        check_vma=False,
    )
```

```python
import math

import jax
import jax.numpy as jnp
from jax import lax
from jax.experimental import pallas as pl
from jax.experimental.pallas import tpu as pltpu
from jax.sharding import PartitionSpec as P

MESH = pl.DeviceIdType.MESH
BF = jnp.bfloat16
F32 = jnp.float32
D = 7168
HALF = D // 2
LAT = 512
LATW = 576
WIDE = 640
HEAD_DIM = 128
POOL_DEV = 96
TOK = 16
BLK = POOL_DEV + TOK
STRETCH = 512
CAP = 12
EIGHTH = D // 8
ROWS = 4 * CAP
TILE = 256
GROUP = 4 * 2 * BLK
NSEC = 8
NEG = -1e30
SCORE = math.log2(math.e) / math.sqrt(192.0)

N_KEY = 31
N_MOE = 31


def one_hot(mask):
    return jnp.where(mask, 1.0, 0.0).astype(BF)


def kernel(
    offset_ref, owner_ref, query_ref, stretch_ref, pool_ref, vup_ref, wo_ref, resid_ref, gain_ref,
    ids_ref, rw_ref, gu_ref, wd_ref,
    out_ref, pages_ref,
    q_raw, qs, keys, acc, ms, ls, ho, wo, wd, gu_raw, w_in, vup, res, gain,
    page_out, part, r_opp, r_rel, r_pure, z_out, z_opp, z_rel, z_pure,
    mid, normed, ss, d_sel, disp, got, hid,
    dpart, e_opp, e_rel, e_pure, e_out, e_got, o_stage,
    load_sem, key_s, key_r, key_x, w_s, w_r, ho_s, ho_r, page_s, page_r,
    ry_s, ry_r, rz_s, rz_r, ss_s, ss_r, moe_s, moe_r, moe_x, hid_s, hid_r,
    ey_s, ey_r, ez_s, ez_r, o_s, o_r,
):
    sec = lax.axis_index("section")
    me = lax.axis_index("expert")
    z = me // 8
    y = (me // 2) % 4
    c = me % 2
    d = 1 - 2 * c
    yp, ym, yo = (y + d + 4) % 4, (y - d + 4) % 4, (y + 2) % 4
    zp, zm, zo = (z + d + 4) % 4, (z - d + 4) % 4, (z + 2) % 4

    def dev(zz, yy, cc):
        return (sec, (zz * 4 + yy) * 2 + cc)

    y_plus, y_minus = dev(z, yp, c), dev(z, ym, c)
    z_plus, z_minus, z_far = dev(zp, y, c), dev(zm, y, c), dev(zo, y, c)
    twin = dev(z, y, 1 - c)
    barrier = pltpu.get_barrier_semaphore()
    for to in (y_plus, y_minus, z_plus, z_minus, z_far, twin):
        pl.semaphore_signal(barrier, inc=1, device_id=to, device_id_type=MESH)
    for k in range(1, NSEC):
        pl.semaphore_signal(barrier, inc=1, device_id=((sec + k) % NSEC, me), device_id_type=MESH)

    def remote(src, dst, s_sem, r_sem, to):
        return pltpu.make_async_remote_copy(
            src_ref=src, dst_ref=dst, send_sem=s_sem, recv_sem=r_sem, device_id=to, device_id_type=MESH
        )

    sent = []

    def send(src, dst, s_sem, r_sem, to):
        copy = remote(src, dst, s_sem, r_sem, to)
        copy.start()
        sent.append(copy)

    def arrived(dst, r_sem):
        remote(dst, dst, r_sem, r_sem, twin).wait_recv()

    half_c = pl.ds(pl.multiple_of(c * HALF, 128), HALF)
    half_x = pl.ds(pl.multiple_of((1 - c) * HALF, 128), HALF)

    wd_c = pl.ds(pl.multiple_of(c * 128, 128), 128)
    wd_x = pl.ds(pl.multiple_of((1 - c) * 128, 128), 128)
    loads = [
        pltpu.make_async_copy(query_ref, q_raw, load_sem.at[0]),
        pltpu.make_async_copy(vup_ref, vup, load_sem.at[1]),
        pltpu.make_async_copy(wo_ref.at[:, half_c], wo.at[c], load_sem.at[2]),
        pltpu.make_async_copy(gu_ref, gu_raw, load_sem.at[3]),
        pltpu.make_async_copy(wd_ref.at[:, half_c], wd.at[wd_c], load_sem.at[4]),
        pltpu.make_async_copy(resid_ref.at[:, half_c], res.at[c], load_sem.at[5]),
        pltpu.make_async_copy(gain_ref.at[:, half_c], gain, load_sem.at[6]),
    ]
    for load in loads:
        load.start()

    lane16 = lax.broadcasted_iota(jnp.int32, (16, 128), 1)
    sub16 = lax.broadcasted_iota(jnp.int32, (16, 128), 0)
    weights = rw_ref[...]
    total = weights[0:1] + weights[1:2]
    share0 = (2.827 * weights[0:1] / total).astype(BF).astype(F32)
    share1 = (2.827 * weights[1:2] / total).astype(BF).astype(F32)
    ids = ids_ref[...]
    which = lax.broadcasted_iota(jnp.int32, (16, TOK), 0)
    table = jnp.where(ids[0:1] == which, share0, 0.0) + jnp.where(ids[1:2] == which, share1, 0.0)
    place = one_hot(lane16 == sub16 + 64)
    tab = jnp.dot(table.astype(BF), place, preferred_element_type=F32).astype(BF)
    mine = pl.ds(pl.multiple_of(c * BLK, 16), BLK)
    first = pl.ds(pl.multiple_of(c * BLK, 16), POOL_DEV)
    last = pl.ds(pl.multiple_of(c * BLK + POOL_DEV, 16), TOK)
    keys[z, y, first, 512:WIDE] = jnp.zeros((POOL_DEV, 128), BF)
    keys[z, y, last, 512:WIDE] = tab
    keys[z, y, first, 0:LATW] = pool_ref[...]
    keys[z, y, last, 0:LATW] = stretch_ref[...]
    latents = stretch_ref[...]
    for g in range(NSEC):
        page_out[g] = jnp.where(owner_ref[0] == g, latents, jnp.zeros_like(latents))

    pl.semaphore_wait(barrier, 6 + NSEC - 1)

    def block(zz, yy):
        return keys.at[zz, yy, mine]

    def key_send(zz, yy, number, to):
        remote(block(zz, yy), block(zz, yy), key_s.at[number], key_r.at[zz, yy], to).start()

    def key_twin(zz, yy, number):
        remote(block(zz, yy), block(zz, yy), key_s.at[number], key_x.at[zz, yy], twin).start()

    def key_wait(zz, yy):
        arrived(block(zz, yy), key_r.at[zz, yy])

    def key_twin_wait(zz, yy):
        theirs = keys.at[zz, yy, pl.ds(pl.multiple_of((1 - c) * BLK, 16), BLK)]
        arrived(theirs, key_x.at[zz, yy])

    key_send(z, y, 2, z_plus)
    key_send(z, y, 3, z_minus)
    key_send(z, y, 0, y_plus)
    key_send(z, y, 1, y_minus)
    key_twin(z, y, 4)
    send(wo_ref.at[:, half_x], wo.at[c], w_s.at[0], w_r.at[0], twin)
    send(wd_ref.at[:, half_x], wd.at[wd_c], w_s.at[1], w_r.at[1], twin)
    send(resid_ref.at[:, half_x], res.at[c], w_s.at[2], w_r.at[2], twin)
    for k in range(1, NSEC):
        g = (sec + k) % NSEC
        send(page_out.at[g], pages_ref.at[sec], page_s.at[k - 1], page_r.at[k - 1], (g, me))
    pages_ref[sec] = page_out[sec]

    loads[0].wait()
    lane = lax.broadcasted_iota(jnp.int32, (STRETCH, WIDE), 1)
    head0 = jnp.where(lane < LATW, q_raw[:, 0:WIDE], jnp.zeros((), BF)).reshape(4, 4, 32, WIDE)
    row_i = lax.broadcasted_iota(jnp.int32, (WIDE, WIDE), 0)
    col_i = lax.broadcasted_iota(jnp.int32, (WIDE, WIDE), 1)
    shift = one_hot((row_i == col_i + 64) & (col_i < LATW))
    head1 = jnp.dot(q_raw[:, 512:1152], shift, preferred_element_type=F32).astype(BF).reshape(4, 4, 32, WIDE)
    for t in range(4):
        qs[t, 0:128] = head0[:, t].reshape(128, WIDE)
        qs[t, 128:256] = head1[:, t].reshape(128, WIDE)
    acc[...] = jnp.zeros_like(acc)
    ls[...] = jnp.zeros_like(ls)
    ms[...] = jnp.full(ms.shape, NEG, F32)

    row_p = lax.broadcasted_iota(jnp.int32, (256, 256), 0)
    col_p = lax.broadcasted_iota(jnp.int32, (256, 256), 1)
    perm = one_hot(jnp.where(row_p < 128, 2 * row_p, 2 * row_p - 255) == col_p)

    def split(i, carry):
        for k in range(4):
            both = gu_raw[pl.ds(pl.multiple_of(i * 1024 + k * 256, 256), 256)]
            out = jnp.dot(perm, both, preferred_element_type=F32).astype(BF)
            rows = pl.ds(pl.multiple_of(i * 512 + k * 128, 128), 128)
            w_in[rows, 0:128] = out[0:128]
            w_in[rows, 128:256] = out[128:256]
        return carry

    def own_column(zz, number):
        key_send(zz, y, number, y_plus)
        key_send(zz, y, number + 1, y_minus)
        key_twin(zz, y, number + 2)

    def key_column(zz, number):
        key_wait(zz, y)
        own_column(zz, number)

    def key_behind(zz, i):
        key_wait(zz, ym)
        key_send(zz, ym, 15 + i, y_plus)
        key_twin(zz, ym, 19 + i)

    def key_ahead(zz, i):
        key_wait(zz, yp)
        key_twin(zz, yp, 23 + i)

    def key_far(zz, i):
        key_wait(zz, yo)
        key_twin(zz, yo, 27 + i)

    def key_ready(blocks):
        for zz, yy in blocks:
            key_twin_wait(zz, yy)

    first_blocks = ((z, y), (z, ym), (z, yp), (zm, y))
    second_blocks = ((zp, y), (zo, y), (z, yo), (zm, ym))
    third_blocks = ((zm, yp), (zp, ym), (zp, yp), (zm, yo))
    last_blocks = ((zo, ym), (zo, yp), (zp, yo), (zo, yo))
    offset = offset_ref[0]

    def attend(blocks, tiles):
        r = lax.broadcasted_iota(jnp.int32, (1, GROUP), 1)
        number = (r >= 2 * BLK).astype(jnp.int32) + (r >= 4 * BLK).astype(jnp.int32) + (r >= 6 * BLK).astype(jnp.int32)
        r = r - number * (2 * BLK)
        cc = (r >= BLK).astype(jnp.int32)
        r = r - cc * BLK
        owner = jnp.zeros_like(r)
        for k, (zz, yy) in enumerate(blocks):
            owner = jnp.where(number == k, zz * 8 + yy * 2 + cc, owner)
        seen = jnp.where(owner * POOL_DEV + r < offset, -1, 1 << 20)
        limit = jnp.where(r < POOL_DEV, seen, owner * TOK + r - POOL_DEV)
        q = lax.broadcasted_iota(jnp.int32, (TILE, 1), 0)
        q = jnp.where(q >= 128, q - 128, q)
        piece = (q >= 32).astype(jnp.int32) + (q >= 64).astype(jnp.int32) + (q >= 96).astype(jnp.int32)
        q = q + 96 * piece
        results = []
        for t in tiles:
            part_keys = jnp.concatenate([keys[zz, yy] for zz, yy in blocks], axis=0)
            s = lax.dot_general(qs[t], part_keys, (((1,), (1,)), ((), ())), preferred_element_type=F32)
            s = jnp.where(limit <= q + 32 * t, s * SCORE, NEG)
            old = ms[t]
            new = jnp.maximum(old, jnp.max(s, axis=1, keepdims=True))
            p = jnp.exp2(s - new[:, 0:1])
            alpha = jnp.exp2(old - new)
            total = ls[t] * alpha + jnp.sum(p, axis=1, keepdims=True)
            add = jnp.dot(p.astype(BF), part_keys[:, 0:LAT], preferred_element_type=F32)
            results.append((new, total, acc[t] * alpha[:, 0:1] + add))
        for t, (new, total, mixed) in zip(tiles, results):
            ms[t] = new
            ls[t] = total
            acc[t] = mixed

    def finish(t, number):
        attend(last_blocks, (t,))
        latent = (acc[t] / ls[t][:, 0:1]).astype(BF)
        for h in range(2):
            head = jnp.dot(latent[h * 128 : h * 128 + 128], vup[h], preferred_element_type=F32).astype(BF)
            ho[c, t, :, h * HEAD_DIM : (h + 1) * HEAD_DIM] = head
        send(ho.at[c, t], ho.at[c, t], ho_s.at[number], ho_r.at[t], twin)

    def project(yy):
        arrived(ho.at[1 - c, yy], ho_r.at[yy])
        left, right = ho[0, yy], ho[1, yy]

        def column(n, carry):
            cols = pl.ds(pl.multiple_of(n * 896, 128), 896)
            out = jnp.dot(left, wo[0, :, cols], preferred_element_type=F32)
            out = out + jnp.dot(right, wo[1, :, cols], preferred_element_type=F32)
            part[yy, :, :, cols] = out.astype(BF).reshape(4, 32, 896)
            return carry

        lax.fori_loop(0, 4, column, 0)

    order = (zo, zm, zp, z)

    def piece(yy, k, h):
        return part.at[yy, order[k], pl.ds(h * TOK, TOK)]

    def opposite(h, k):
        send(piece(yo, k, h), r_opp.at[h, k], ry_s.at[h, k], ry_r.at[h, k], y_plus)

    def behind(h, k):
        send(piece(ym, k, h), r_pure.at[h, k], ry_s.at[h, 4 + k], ry_r.at[h, 4 + k], y_minus)

    def onward(h, k):
        arrived(r_opp.at[h, k], ry_r.at[h, k])
        at = piece(yp, k, h)
        at[...] = (at[...].astype(F32) + r_opp[h, k].astype(F32)).astype(BF)
        send(at, r_rel.at[h, k], ry_s.at[h, 8 + k], ry_r.at[h, 8 + k], y_plus)

    def column_sum(h, k):
        arrived(r_pure.at[h, k], ry_r.at[h, 4 + k])
        arrived(r_rel.at[h, k], ry_r.at[h, 8 + k])
        return piece(y, k, h)[...].astype(F32) + r_rel[h, k].astype(F32) + r_pure[h, k].astype(F32)

    lane_r = lax.broadcasted_iota(jnp.int32, (128, 128), 0)
    lane_c = lax.broadcasted_iota(jnp.int32, (128, 128), 1)
    earlier = one_hot((lane_r < lane_c) & (lane_c < TOK))

    def routes(h, zz, yy):
        at = h * BLK + POOL_DEV
        tail = keys[zz, yy, at : at + TOK, 512:WIDE].astype(F32)
        shares = jnp.where(lane16 < TOK, pltpu.roll(tail, 64, 1), 0.0)
        chosen = shares > 0.0
        rank = jnp.dot(one_hot(chosen), earlier, preferred_element_type=F32)
        return shares, jnp.where(chosen, rank, -1.0)

    def quarter_of(r):
        return jnp.where(r < 32, jnp.right_shift(r, 3), jnp.right_shift(r - 32, 2))

    def slot_of(r):
        return jnp.where(r < 32, jnp.bitwise_and(r, 7), 8 + jnp.bitwise_and(r, 3))

    row48 = lax.broadcasted_iota(jnp.int32, (ROWS, 128), 0)
    slot48 = slot_of(row48).astype(F32)
    quarter48 = quarter_of(row48)
    row16 = jnp.where(sub16 < 8, sub16, 8 + jnp.bitwise_and(sub16, 3)).astype(F32)
    quarter_all = quarter_of(lax.broadcasted_iota(jnp.int32, (4, ROWS, 1), 1)).reshape(4 * ROWS, 1)

    def pick_rows():
        for h in range(2):
            _, own_slot = routes(h, z, y)
            for e in range(4):
                hit = own_slot[e : e + 1] == slot48
                for j in range(4):
                    d_sel[h, j, e * ROWS : (e + 1) * ROWS] = one_hot(hit & (quarter48 == j))

    def z_first(h):
        z_out[h, 0] = column_sum(h, 0).astype(BF)
        send(z_out.at[h, 0], z_opp.at[h], rz_s.at[h, 0], rz_r.at[h, 0], z_plus)

    def z_second(h):
        z_out[h, 1] = column_sum(h, 1).astype(BF)
        send(z_out.at[h, 1], z_pure.at[h], rz_s.at[h, 1], rz_r.at[h, 1], z_minus)

    def z_third(h):
        ahead = column_sum(h, 2)
        arrived(z_opp.at[h], rz_r.at[h, 0])
        z_out[h, 2] = (ahead + z_opp[h].astype(F32)).astype(BF)
        send(z_out.at[h, 2], z_rel.at[h], rz_s.at[h, 2], rz_r.at[h, 2], z_plus)

    def norm(h):
        middle = column_sum(h, 3) + res[h].astype(F32)
        arrived(z_pure.at[h], rz_r.at[h, 1])
        arrived(z_rel.at[h], rz_r.at[h, 2])
        middle = middle + z_pure[h].astype(F32) + z_rel[h].astype(F32)
        mid[h] = middle
        ss[h, 0] = jnp.broadcast_to(jnp.sum(middle * middle, axis=1, keepdims=True), (TOK, 128))
        send(ss.at[h, 0], ss.at[h, 1], ss_s.at[h], ss_r.at[h], twin)

    def slab(h, zz, yy):
        return got.at[h, c, zz, yy]

    def moe_send(h, zz, yy, number, to):
        remote(slab(h, zz, yy), slab(h, zz, yy), moe_s.at[h, number], moe_r.at[h, zz, yy], to).start()

    def moe_twin(h, zz, yy, number):
        remote(slab(h, zz, yy), slab(h, zz, yy), moe_s.at[h, number], moe_x.at[h, zz, yy], twin).start()

    def moe_wait(h, zz, yy):
        arrived(slab(h, zz, yy), moe_r.at[h, zz, yy])

    def moe_column(h, zz, number):
        moe_send(h, zz, y, number, y_plus)
        moe_send(h, zz, y, number + 1, y_minus)
        moe_twin(h, zz, y, number + 2)

    def dispatch(h):
        arrived(ss.at[h, 1], ss_r.at[h])
        scale = lax.rsqrt((ss[h, 0] + ss[h, 1])[:, 0:1] * (1.0 / D) + 1e-06)
        normed[h] = (mid[h] * scale * gain[...]).astype(BF)
        out = jnp.zeros((4 * ROWS, EIGHTH), F32)
        for j in range(4):
            cols = normed[h, :, j * EIGHTH : (j + 1) * EIGHTH]
            out = out + jnp.dot(d_sel[h, j, :, 0:TOK], cols, preferred_element_type=F32)
        disp[h] = out.astype(BF).reshape(4, ROWS, EIGHTH)
        remote(disp.at[h, zp], slab(h, z, y), moe_s.at[h, 1], moe_r.at[h, z, y], z_plus).start()
        remote(disp.at[h, zm], slab(h, z, y), moe_s.at[h, 2], moe_r.at[h, z, y], z_minus).start()
        remote(disp.at[h, zo], slab(h, z, y), moe_s.at[h, 0], moe_r.at[h, z, y], z_far).start()
        got[h, c, z, y] = disp[h, z]
        moe_column(h, z, 3)

    def moe_spread(h, zz, number):
        moe_wait(h, zz, y)
        moe_column(h, zz, number)

    def moe_behind(h, zz, i):
        moe_wait(h, zz, ym)
        moe_send(h, zz, ym, 15 + i, y_plus)
        moe_twin(h, zz, ym, 19 + i)

    def moe_ahead(h, zz, i):
        moe_wait(h, zz, yp)
        moe_twin(h, zz, yp, 23 + i)

    def moe_far(h, zz, i):
        moe_wait(h, zz, yo)
        moe_twin(h, zz, yo, 27 + i)

    def experts(h, yy, number):
        for zz in (z, zm, zp, zo):
            arrived(got.at[h, 1 - c, zz, yy], moe_x.at[h, zz, yy])
        first_rows = got[h, 0, :, yy].reshape(4 * ROWS, EIGHTH)
        second_rows = got[h, 1, :, yy].reshape(4 * ROWS, EIGHTH)
        picked = jnp.zeros((4 * ROWS, 256), F32)
        for j in range(4):
            at = j * EIGHTH
            out = jnp.dot(first_rows, w_in[at : at + EIGHTH], preferred_element_type=F32)
            out = out + jnp.dot(second_rows, w_in[HALF + at : HALF + at + EIGHTH], preferred_element_type=F32)
            picked = jnp.where(quarter_all == j, out, picked)
        for zz in range(4):
            at = zz * ROWS
            head = picked[at : at + 8] + picked[at + 8 : at + 16] + picked[at + 16 : at + 24] + picked[at + 24 : at + 32]
            tail = picked[at + 32 : at + 40] + picked[at + 40 : at + 48]
            tail = tail + pltpu.roll(tail, 4, 0)
            both = jnp.concatenate([head, tail], axis=0)
            gate, upper = both[:, 0:128], both[:, 128:256]
            shares, slot = routes(h, zz, yy)
            mine_e = sub16 == z
            share = jnp.sum(jnp.where(mine_e, shares, 0.0), axis=0, keepdims=True)
            place_e = jnp.sum(jnp.where(mine_e, slot, 0.0), axis=0, keepdims=True)
            factor = jnp.sum(jnp.where(place_e == row16, share, 0.0), axis=1, keepdims=True)
            hidden = factor * (gate * (1.0 / (1.0 + jnp.exp(-gate))) * upper)
            low, high = hidden[0:8], hidden[8:16]
            hid[h, yy, at : at + ROWS, wd_c] = jnp.concatenate([low, low, low, low, high, high], axis=0).astype(BF)
        here = hid.at[h, yy, :, wd_c]
        remote(here, here, hid_s.at[h, number], hid_r.at[h, yy], twin).start()

    def down(h, yy):
        arrived(hid.at[h, yy, :, wd_x], hid_r.at[h, yy])
        rows = hid[h, yy]
        out = jnp.zeros((4 * ROWS, EIGHTH), F32)
        for j in range(4):
            term = jnp.dot(rows, wd[:, j * EIGHTH : (j + 1) * EIGHTH], preferred_element_type=F32)
            out = jnp.where(quarter_all == j, term, out)
        dpart[h, yy] = out.astype(BF).reshape(4, ROWS, EIGHTH)

    def e_behind(h, k):
        send(dpart.at[h, ym, order[k]], e_pure.at[h, k], ey_s.at[h, 4 + k], ey_r.at[h, 4 + k], y_minus)

    def e_opposite(h, k):
        send(dpart.at[h, yo, order[k]], e_opp.at[h, k], ey_s.at[h, k], ey_r.at[h, k], y_plus)

    def e_onward(h, k):
        arrived(e_opp.at[h, k], ey_r.at[h, k])
        dpart[h, yp, order[k]] = (dpart[h, yp, order[k]].astype(F32) + e_opp[h, k].astype(F32)).astype(BF)
        send(dpart.at[h, yp, order[k]], e_rel.at[h, k], ey_s.at[h, 8 + k], ey_r.at[h, 8 + k], y_plus)

    def plane_sum(h, k):
        arrived(e_pure.at[h, k], ey_r.at[h, 4 + k])
        arrived(e_rel.at[h, k], ey_r.at[h, 8 + k])
        s = dpart[h, y, order[k]].astype(F32) + e_rel[h, k].astype(F32) + e_pure[h, k].astype(F32)
        return s.astype(BF)

    def back_first(h):
        e_out[h, 0] = plane_sum(h, 0)
        send(e_out.at[h, 0], e_got.at[h, z], ez_s.at[h, 0], ez_r.at[h, z], z_far)

    def back_second(h):
        e_out[h, 1] = plane_sum(h, 1)
        send(e_out.at[h, 1], e_got.at[h, z], ez_s.at[h, 1], ez_r.at[h, z], z_minus)

    def back_third(h):
        e_out[h, 2] = plane_sum(h, 2)
        send(e_out.at[h, 2], e_got.at[h, z], ez_s.at[h, 2], ez_r.at[h, z], z_plus)

    def combine(h):
        e_got[h, z] = plane_sum(h, 3)
        for zz in (zm, zp, zo):
            arrived(e_got.at[h, zz], ez_r.at[h, zz])
        rows = e_got[h].reshape(4 * ROWS, EIGHTH)
        for j in range(4):
            pick = d_sel[h, j, :, 0:TOK]
            moe = lax.dot_general(pick, rows, (((0,), (0,)), ((), ())), preferred_element_type=F32)
            at = j * EIGHTH
            o_stage[h, :, at : at + EIGHTH] = (mid[h, :, at : at + EIGHTH] + moe).astype(BF)

    loads[3].wait()
    lax.fori_loop(0, D // 512, split, 0)
    key_behind(z, 0)
    key_ahead(z, 0)
    key_wait(zm, y)
    key_send(zm, y, 5, z_plus)
    own_column(zm, 6)
    key_column(zp, 9)
    key_ready(first_blocks)
    attend(first_blocks, (2, 3))
    key_far(z, 0)
    attend(first_blocks, (0, 1))
    key_behind(zm, 1)
    key_column(zo, 12)
    key_ahead(zm, 1)
    key_behind(zp, 2)
    key_ahead(zp, 2)
    key_ready(second_blocks)
    attend(second_blocks, (2, 3))
    key_behind(zo, 3)
    key_far(zm, 1)
    attend(second_blocks, (0, 1))
    key_ahead(zo, 3)
    key_far(zp, 2)
    key_ready(third_blocks)
    attend(third_blocks, (0, 1))
    key_far(zo, 3)
    attend(third_blocks, (2, 3))
    key_ready(last_blocks)
    loads[1].wait()
    finish(yo, 3)
    finish(ym, 1)
    loads[2].wait()
    arrived(wo.at[1 - c], w_r.at[0])
    project(yo)
    opposite(1, 1)
    opposite(0, 1)
    opposite(1, 0)
    opposite(0, 0)
    opposite(1, 2)
    finish(y, 0)
    opposite(1, 3)
    pick_rows()
    opposite(0, 2)
    finish(yp, 2)
    project(yp)
    onward(1, 0)
    project(ym)
    behind(1, 0)
    onward(0, 0)
    behind(0, 0)
    behind(1, 1)
    onward(1, 1)
    behind(1, 2)
    onward(1, 2)
    behind(0, 2)
    behind(1, 3)
    project(y)
    onward(0, 2)
    onward(1, 3)
    onward(0, 1)
    behind(0, 1)
    behind(0, 3)
    opposite(0, 3)
    z_first(1)
    z_first(0)
    z_second(1)
    z_third(1)
    z_third(0)
    loads[5].wait()
    loads[6].wait()
    arrived(res.at[1 - c], w_r.at[2])
    norm(1)
    z_second(0)
    dispatch(1)
    onward(0, 3)
    moe_behind(1, z, 0)
    moe_ahead(1, z, 0)
    norm(0)
    moe_spread(1, zm, 6)
    moe_far(1, z, 0)
    dispatch(0)
    moe_spread(1, zp, 9)
    moe_behind(1, zm, 1)
    moe_ahead(1, zm, 1)
    moe_behind(0, z, 0)
    moe_ahead(0, z, 0)
    moe_spread(1, zo, 12)
    moe_behind(1, zp, 2)
    moe_spread(0, zm, 6)
    moe_ahead(1, zp, 2)
    experts(1, y, 0)
    moe_spread(0, zp, 9)
    moe_far(0, z, 0)
    moe_far(1, zm, 1)
    loads[4].wait()
    arrived(wd.at[wd_x], w_r.at[1])
    down(1, y)
    moe_behind(1, zo, 3)
    moe_ahead(1, zo, 3)
    moe_far(1, zp, 2)
    experts(1, yp, 2)
    moe_spread(0, zo, 12)
    moe_ahead(0, zm, 1)
    experts(1, ym, 1)
    moe_behind(0, zp, 2)
    moe_ahead(0, zp, 2)
    down(1, ym)
    e_behind(1, 2)
    e_behind(1, 1)
    e_behind(1, 0)
    moe_far(1, zo, 3)
    moe_behind(0, zm, 1)
    e_behind(1, 3)
    moe_behind(0, zo, 3)
    down(1, yp)
    moe_ahead(0, zo, 3)
    experts(1, yo, 3)
    experts(0, yp, 2)
    down(1, yo)
    e_opposite(1, 2)
    e_opposite(1, 1)
    e_opposite(1, 3)
    e_opposite(1, 0)
    moe_far(0, zp, 2)
    experts(0, ym, 1)
    moe_far(0, zm, 1)
    down(0, ym)
    e_behind(0, 2)
    e_behind(0, 3)
    moe_far(0, zo, 3)
    down(0, yp)
    e_behind(0, 1)
    e_onward(1, 2)
    e_behind(0, 0)
    e_onward(1, 1)
    experts(0, yo, 3)
    e_onward(1, 3)
    e_onward(1, 0)
    experts(0, y, 0)
    down(0, yo)
    e_opposite(0, 2)
    e_opposite(0, 0)
    e_opposite(0, 1)
    e_opposite(0, 3)
    down(0, y)
    back_third(1)
    back_second(1)
    back_first(1)
    e_onward(0, 2)
    e_onward(0, 0)
    e_onward(0, 1)
    e_onward(0, 3)
    back_third(0)
    back_first(0)
    back_second(0)
    combine(1)
    combine(0)
    send(o_stage.at[1 - c], out_ref.at[:, half_c], o_s.at[0], o_r.at[0], twin)
    out_ref[:, half_c] = o_stage[c]
    arrived(out_ref.at[:, half_x], o_r.at[0])

    for k in range(1, NSEC):
        g = (sec - k + NSEC) % NSEC
        arrived(pages_ref.at[g], page_r.at[k - 1])
    for copy in sent:
        copy.wait_send()

    def key_done(i, carry):
        remote(block(z, y), block(z, y), key_s.at[i], key_r.at[z, y], twin).wait_send()
        return carry

    lax.fori_loop(0, N_KEY, key_done, 0)

    def moe_done(i, carry):
        for h in range(2):
            remote(slab(h, z, y), slab(h, z, y), moe_s.at[h, i], moe_r.at[h, z, y], twin).wait_send()
        return carry

    lax.fori_loop(0, N_MOE, moe_done, 0)

    def hid_done(i, carry):
        for h in range(2):
            here = hid.at[h, i, :, wd_c]
            remote(here, here, hid_s.at[h, i], hid_r.at[h, i], twin).wait_send()
        return carry

    lax.fori_loop(0, 4, hid_done, 0)


def body(
    queries, stretch_latents, pool_latents, stretch_offset, value_up, out_proj, resid, norm_gain,
    expert_ids, route_weight, gate_up, down_proj, page_owner,
):
    anywhere = pl.BlockSpec(memory_space=pl.ANY)
    vmem = pl.BlockSpec(memory_space=pltpu.VMEM)
    smem = pl.BlockSpec(memory_space=pltpu.SMEM)
    V = pltpu.VMEM
    S = lambda *shape: pltpu.SemaphoreType.DMA(shape)
    scratch = [
        V((STRETCH, 2 * LATW), BF), V((4, TILE, WIDE), BF), V((4, 4, 2 * BLK, WIDE), BF),
        V((4, TILE, LAT), F32), V((4, TILE, 128), F32), V((4, TILE, 128), F32),
        V((2, 4, 128, 256), BF), V((2, 256, HALF), BF), V((256, HALF), BF),
        V((2 * D, 128), BF), V((D, 256), BF), V((2, LAT, HEAD_DIM), BF),
        V((2, TOK, HALF), BF), V((1, HALF), F32),
        V((NSEC, TOK, LATW), BF), V((4, 4, 32, HALF), BF),
        V((2, 4, TOK, HALF), BF), V((2, 4, TOK, HALF), BF), V((2, 4, TOK, HALF), BF),
        V((2, 3, TOK, HALF), BF), V((2, TOK, HALF), BF), V((2, TOK, HALF), BF), V((2, TOK, HALF), BF),
        V((2, TOK, HALF), F32), V((2, TOK, HALF), BF), V((2, 2, TOK, 128), F32),
        V((2, 4, 4 * ROWS, 128), BF),
        V((2, 4, ROWS, EIGHTH), BF), V((2, 2, 4, 4, ROWS, EIGHTH), BF),
        V((2, 4, 4 * ROWS, 256), BF),
        V((2, 4, 4, ROWS, EIGHTH), BF),
        V((2, 4, ROWS, EIGHTH), BF), V((2, 4, ROWS, EIGHTH), BF), V((2, 4, ROWS, EIGHTH), BF),
        V((2, 3, ROWS, EIGHTH), BF), V((2, 4, ROWS, EIGHTH), BF),
        V((2, TOK, HALF), BF),
        S(7), S(N_KEY), S(4, 4), S(4, 4), S(3), S(3), S(4), S(4), S(7), S(7),
        S(2, 12), S(2, 12), S(2, 3), S(2, 3), S(2), S(2),
        S(2, N_MOE), S(2, 4, 4), S(2, 4, 4), S(2, 4), S(2, 4),
        S(2, 12), S(2, 12), S(2, 3), S(2, 4), S(1), S(1),
    ]
    out, pages = pl.pallas_call(
        kernel,
        out_shape=(
            jax.ShapeDtypeStruct((TOK, D), BF),
            jax.ShapeDtypeStruct((NSEC, TOK, LATW), BF),
        ),
        in_specs=[smem, smem, anywhere, vmem, vmem, anywhere, anywhere, anywhere, anywhere, vmem, vmem, anywhere, anywhere],
        out_specs=(vmem, vmem),
        scratch_shapes=scratch,
        compiler_params=pltpu.CompilerParams(
            collective_id=0, has_side_effects=True, vmem_limit_bytes=60 * 1024 * 1024
        ),
    )(
        stretch_offset,
        page_owner[0],
        queries[0],
        stretch_latents[0],
        pool_latents[0],
        value_up[0],
        out_proj[0],
        resid[0],
        norm_gain,
        expert_ids[0].T,
        route_weight[0].T,
        gate_up[0, 0].reshape(2 * D, 128),
        down_proj[0, 0],
    )
    return out[None], pages.reshape(1, 1, NSEC, TOK * LATW)


def solution(mesh):
    placed = (
        P("section", None, "expert"),
        P("section", "expert", None),
        P("section", "expert", None),
        P("section"),
        P("section", "expert", None, None),
        P("section", "expert", None),
        P("section", "expert", None),
        P("section", None),
        P("section", "expert", None),
        P("section", "expert", None),
        P("section", "expert", None, None, None),
        P("section", "expert", None, None),
        P("section", "expert"),
    )
    return jax.shard_map(
        body,
        mesh=mesh,
        in_specs=placed,
        out_specs=(P("section", "expert", None), P("section", "expert", None, None)),
        check_vma=False,
    )
```

```python
import math

import jax
import jax.numpy as jnp
from jax import lax
from jax.experimental import pallas as pl
from jax.experimental.pallas import tpu as pltpu
from jax.sharding import PartitionSpec as P

MESH = pl.DeviceIdType.MESH
BF = jnp.bfloat16
F32 = jnp.float32
D = 7168
HALF = D // 2
LAT = 512
LATW = 576
WIDE = 640
HEAD_DIM = 128
POOL_DEV = 96
TOK = 16
BLK = POOL_DEV + TOK
STRETCH = 512
CAP = 12
EIGHTH = D // 8
ROWS = 4 * CAP
TILE = 256
GROUP = 4 * 2 * BLK
NSEC = 8
NEG = -1e30
SCORE = math.log2(math.e) / math.sqrt(192.0)

N_KEY = 31
N_MOE = 31


def one_hot(mask):
    return jnp.where(mask, 1.0, 0.0).astype(BF)


def kernel(
    offset_ref, owner_ref, query_ref, stretch_ref, pool_ref, vup_ref, wo_ref, resid_ref, gain_ref,
    ids_ref, rw_ref, gu_ref, wd_ref,
    out_ref, pages_ref,
    q_raw, qs, keys, acc, ms, ls, ho, wo, wd, gu_raw, w_in, vup, res, gain,
    page_out, part, r_opp, r_rel, r_pure, z_out, z_opp, z_rel, z_pure,
    mid, normed, ss, d_sel, disp, got, hid,
    dpart, e_opp, e_rel, e_pure, e_out, e_got, o_stage,
    load_sem, key_s, key_r, key_x, w_s, w_r, ho_s, ho_r, page_s, page_r,
    ry_s, ry_r, rz_s, rz_r, ss_s, ss_r, moe_s, moe_r, moe_x, hid_s, hid_r,
    ey_s, ey_r, ez_s, ez_r, o_s, o_r,
):
    sec = lax.axis_index("section")
    me = lax.axis_index("expert")
    z = me // 8
    y = (me // 2) % 4
    c = me % 2
    d = 1 - 2 * c
    yp, ym, yo = (y + d + 4) % 4, (y - d + 4) % 4, (y + 2) % 4
    zp, zm, zo = (z + d + 4) % 4, (z - d + 4) % 4, (z + 2) % 4

    def dev(zz, yy, cc):
        return (sec, (zz * 4 + yy) * 2 + cc)

    y_plus, y_minus = dev(z, yp, c), dev(z, ym, c)
    z_plus, z_minus, z_far = dev(zp, y, c), dev(zm, y, c), dev(zo, y, c)
    twin = dev(z, y, 1 - c)
    barrier = pltpu.get_barrier_semaphore()
    for to in (y_plus, y_minus, z_plus, z_minus, z_far, twin):
        pl.semaphore_signal(barrier, inc=1, device_id=to, device_id_type=MESH)
    for k in range(1, NSEC):
        pl.semaphore_signal(barrier, inc=1, device_id=((sec + k) % NSEC, me), device_id_type=MESH)

    def remote(src, dst, s_sem, r_sem, to):
        return pltpu.make_async_remote_copy(
            src_ref=src, dst_ref=dst, send_sem=s_sem, recv_sem=r_sem, device_id=to, device_id_type=MESH
        )

    sent = []

    def send(src, dst, s_sem, r_sem, to):
        copy = remote(src, dst, s_sem, r_sem, to)
        copy.start()
        sent.append(copy)

    def arrived(dst, r_sem):
        remote(dst, dst, r_sem, r_sem, twin).wait_recv()

    half_c = pl.ds(pl.multiple_of(c * HALF, 128), HALF)
    half_x = pl.ds(pl.multiple_of((1 - c) * HALF, 128), HALF)

    wd_c = pl.ds(pl.multiple_of(c * 128, 128), 128)
    wd_x = pl.ds(pl.multiple_of((1 - c) * 128, 128), 128)
    loads = [
        pltpu.make_async_copy(query_ref, q_raw, load_sem.at[0]),
        pltpu.make_async_copy(vup_ref, vup, load_sem.at[1]),
        pltpu.make_async_copy(wo_ref.at[:, half_c], wo.at[c], load_sem.at[2]),
        pltpu.make_async_copy(gu_ref, gu_raw, load_sem.at[3]),
        pltpu.make_async_copy(wd_ref.at[:, half_c], wd.at[wd_c], load_sem.at[4]),
        pltpu.make_async_copy(resid_ref.at[:, half_c], res.at[c], load_sem.at[5]),
        pltpu.make_async_copy(gain_ref.at[:, half_c], gain, load_sem.at[6]),
    ]
    for load in loads:
        load.start()

    lane16 = lax.broadcasted_iota(jnp.int32, (16, 128), 1)
    sub16 = lax.broadcasted_iota(jnp.int32, (16, 128), 0)
    weights = rw_ref[...]
    total = weights[0:1] + weights[1:2]
    share0 = (2.827 * weights[0:1] / total).astype(BF).astype(F32)
    share1 = (2.827 * weights[1:2] / total).astype(BF).astype(F32)
    ids = ids_ref[...]
    which = lax.broadcasted_iota(jnp.int32, (16, TOK), 0)
    table = jnp.where(ids[0:1] == which, share0, 0.0) + jnp.where(ids[1:2] == which, share1, 0.0)
    place = one_hot(lane16 == sub16 + 64)
    tab = jnp.dot(table.astype(BF), place, preferred_element_type=F32).astype(BF)
    mine = pl.ds(pl.multiple_of(c * BLK, 16), BLK)
    first = pl.ds(pl.multiple_of(c * BLK, 16), POOL_DEV)
    last = pl.ds(pl.multiple_of(c * BLK + POOL_DEV, 16), TOK)
    keys[z, y, first, 512:WIDE] = jnp.zeros((POOL_DEV, 128), BF)
    keys[z, y, last, 512:WIDE] = tab
    keys[z, y, first, 0:LATW] = pool_ref[...]
    keys[z, y, last, 0:LATW] = stretch_ref[...]
    latents = stretch_ref[...]
    for g in range(NSEC):
        page_out[g] = jnp.where(owner_ref[0] == g, latents, jnp.zeros_like(latents))

    pl.semaphore_wait(barrier, 6 + NSEC - 1)

    def block(zz, yy):
        return keys.at[zz, yy, mine]

    def key_send(zz, yy, number, to):
        remote(block(zz, yy), block(zz, yy), key_s.at[number], key_r.at[zz, yy], to).start()

    def key_twin(zz, yy, number):
        remote(block(zz, yy), block(zz, yy), key_s.at[number], key_x.at[zz, yy], twin).start()

    def key_wait(zz, yy):
        arrived(block(zz, yy), key_r.at[zz, yy])

    def key_twin_wait(zz, yy):
        theirs = keys.at[zz, yy, pl.ds(pl.multiple_of((1 - c) * BLK, 16), BLK)]
        arrived(theirs, key_x.at[zz, yy])

    key_send(z, y, 2, z_plus)
    key_send(z, y, 3, z_minus)
    key_send(z, y, 0, y_plus)
    key_send(z, y, 1, y_minus)
    key_twin(z, y, 4)
    send(wo_ref.at[:, half_x], wo.at[c], w_s.at[0], w_r.at[0], twin)
    send(wd_ref.at[:, half_x], wd.at[wd_c], w_s.at[1], w_r.at[1], twin)
    send(resid_ref.at[:, half_x], res.at[c], w_s.at[2], w_r.at[2], twin)
    for k in range(1, NSEC):
        g = (sec + k) % NSEC
        send(page_out.at[g], pages_ref.at[sec], page_s.at[k - 1], page_r.at[k - 1], (g, me))
    pages_ref[sec] = page_out[sec]

    loads[0].wait()
    lane = lax.broadcasted_iota(jnp.int32, (STRETCH, WIDE), 1)
    head0 = jnp.where(lane < LATW, q_raw[:, 0:WIDE], jnp.zeros((), BF)).reshape(4, 4, 32, WIDE)
    row_i = lax.broadcasted_iota(jnp.int32, (WIDE, WIDE), 0)
    col_i = lax.broadcasted_iota(jnp.int32, (WIDE, WIDE), 1)
    shift = one_hot((row_i == col_i + 64) & (col_i < LATW))
    head1 = jnp.dot(q_raw[:, 512:1152], shift, preferred_element_type=F32).astype(BF).reshape(4, 4, 32, WIDE)
    for t in range(4):
        qs[t, 0:128] = head0[:, t].reshape(128, WIDE)
        qs[t, 128:256] = head1[:, t].reshape(128, WIDE)
    acc[...] = jnp.zeros_like(acc)
    ls[...] = jnp.zeros_like(ls)
    ms[...] = jnp.full(ms.shape, NEG, F32)

    row_p = lax.broadcasted_iota(jnp.int32, (256, 256), 0)
    col_p = lax.broadcasted_iota(jnp.int32, (256, 256), 1)
    perm = one_hot(jnp.where(row_p < 128, 2 * row_p, 2 * row_p - 255) == col_p)

    def split(i, carry):
        for k in range(4):
            both = gu_raw[pl.ds(pl.multiple_of(i * 1024 + k * 256, 256), 256)]
            out = jnp.dot(perm, both, preferred_element_type=F32).astype(BF)
            rows = pl.ds(pl.multiple_of(i * 512 + k * 128, 128), 128)
            w_in[rows, 0:128] = out[0:128]
            w_in[rows, 128:256] = out[128:256]
        return carry

    def own_column(zz, number):
        key_send(zz, y, number, y_plus)
        key_send(zz, y, number + 1, y_minus)
        key_twin(zz, y, number + 2)

    def key_column(zz, number):
        key_wait(zz, y)
        own_column(zz, number)

    def key_behind(zz, i):
        key_wait(zz, ym)
        key_send(zz, ym, 15 + i, y_plus)
        key_twin(zz, ym, 19 + i)

    def key_ahead(zz, i):
        key_wait(zz, yp)
        key_twin(zz, yp, 23 + i)

    def key_far(zz, i):
        key_wait(zz, yo)
        key_twin(zz, yo, 27 + i)

    def key_ready(blocks):
        for zz, yy in blocks:
            key_twin_wait(zz, yy)

    first_blocks = ((z, y), (z, ym), (z, yp), (zm, y))
    second_blocks = ((zp, y), (zo, y), (z, yo), (zm, ym))
    third_blocks = ((zm, yp), (zp, ym), (zp, yp), (zm, yo))
    last_blocks = ((zo, ym), (zo, yp), (zp, yo), (zo, yo))
    offset = offset_ref[0]

    def attend(blocks, tiles):
        r = lax.broadcasted_iota(jnp.int32, (1, GROUP), 1)
        number = (r >= 2 * BLK).astype(jnp.int32) + (r >= 4 * BLK).astype(jnp.int32) + (r >= 6 * BLK).astype(jnp.int32)
        r = r - number * (2 * BLK)
        cc = (r >= BLK).astype(jnp.int32)
        r = r - cc * BLK
        owner = jnp.zeros_like(r)
        for k, (zz, yy) in enumerate(blocks):
            owner = jnp.where(number == k, zz * 8 + yy * 2 + cc, owner)
        seen = jnp.where(owner * POOL_DEV + r < offset, -1, 1 << 20)
        limit = jnp.where(r < POOL_DEV, seen, owner * TOK + r - POOL_DEV)
        q = lax.broadcasted_iota(jnp.int32, (TILE, 1), 0)
        q = jnp.where(q >= 128, q - 128, q)
        piece = (q >= 32).astype(jnp.int32) + (q >= 64).astype(jnp.int32) + (q >= 96).astype(jnp.int32)
        q = q + 96 * piece
        span = len(tiles)
        at = pl.ds(tiles[0], span)
        part_keys = jnp.concatenate([keys[zz, yy] for zz, yy in blocks], axis=0)
        token = jnp.concatenate([q + 32 * t for t in tiles], axis=0)
        many = qs[at].reshape(span * TILE, WIDE)
        s = lax.dot_general(many, part_keys, (((1,), (1,)), ((), ())), preferred_element_type=F32)
        s = jnp.where(limit <= token, s * SCORE, NEG)
        old = ms[at].reshape(span * TILE, 128)
        new = jnp.maximum(old, jnp.max(s, axis=1, keepdims=True))
        p = jnp.exp2(s - new[:, 0:1])
        alpha = jnp.exp2(old - new)
        ms[at] = new.reshape(span, TILE, 128)
        total = ls[at].reshape(span * TILE, 128) * alpha + jnp.sum(p, axis=1, keepdims=True)
        ls[at] = total.reshape(span, TILE, 128)
        add = jnp.dot(p.astype(BF), part_keys[:, 0:LAT], preferred_element_type=F32)
        acc[at] = (acc[at].reshape(span * TILE, LAT) * alpha[:, 0:1] + add).reshape(span, TILE, LAT)

    def finish(t, number):
        attend(last_blocks, (t,))
        latent = (acc[t] / ls[t][:, 0:1]).astype(BF)
        for h in range(2):
            head = jnp.dot(latent[h * 128 : h * 128 + 128], vup[h], preferred_element_type=F32).astype(BF)
            ho[c, t, :, h * HEAD_DIM : (h + 1) * HEAD_DIM] = head
        send(ho.at[c, t], ho.at[c, t], ho_s.at[number], ho_r.at[t], twin)

    def project(yy):
        arrived(ho.at[1 - c, yy], ho_r.at[yy])
        left, right = ho[0, yy], ho[1, yy]

        def column(n, carry):
            cols = pl.ds(pl.multiple_of(n * 896, 128), 896)
            out = jnp.dot(left, wo[0, :, cols], preferred_element_type=F32)
            out = out + jnp.dot(right, wo[1, :, cols], preferred_element_type=F32)
            part[yy, :, :, cols] = out.astype(BF).reshape(4, 32, 896)
            return carry

        lax.fori_loop(0, 4, column, 0)

    order = (zo, zm, zp, z)

    def piece(yy, k, h):
        return part.at[yy, order[k], pl.ds(h * TOK, TOK)]

    def opposite(h, k):
        send(piece(yo, k, h), r_opp.at[h, k], ry_s.at[h, k], ry_r.at[h, k], y_plus)

    def behind(h, k):
        send(piece(ym, k, h), r_pure.at[h, k], ry_s.at[h, 4 + k], ry_r.at[h, 4 + k], y_minus)

    def onward(h, k):
        arrived(r_opp.at[h, k], ry_r.at[h, k])
        at = piece(yp, k, h)
        at[...] = (at[...].astype(F32) + r_opp[h, k].astype(F32)).astype(BF)
        send(at, r_rel.at[h, k], ry_s.at[h, 8 + k], ry_r.at[h, 8 + k], y_plus)

    def column_sum(h, k):
        arrived(r_pure.at[h, k], ry_r.at[h, 4 + k])
        arrived(r_rel.at[h, k], ry_r.at[h, 8 + k])
        return piece(y, k, h)[...].astype(F32) + r_rel[h, k].astype(F32) + r_pure[h, k].astype(F32)

    lane_r = lax.broadcasted_iota(jnp.int32, (128, 128), 0)
    lane_c = lax.broadcasted_iota(jnp.int32, (128, 128), 1)
    earlier = one_hot((lane_r < lane_c) & (lane_c < TOK))

    def routes(h, zz, yy):
        at = h * BLK + POOL_DEV
        tail = keys[zz, yy, at : at + TOK, 512:WIDE].astype(F32)
        shares = jnp.where(lane16 < TOK, pltpu.roll(tail, 64, 1), 0.0)
        chosen = shares > 0.0
        rank = jnp.dot(one_hot(chosen), earlier, preferred_element_type=F32)
        return shares, jnp.where(chosen, rank, -1.0)

    def quarter_of(r):
        return jnp.where(r < 32, jnp.right_shift(r, 3), jnp.right_shift(r - 32, 2))

    def slot_of(r):
        return jnp.where(r < 32, jnp.bitwise_and(r, 7), 8 + jnp.bitwise_and(r, 3))

    row48 = lax.broadcasted_iota(jnp.int32, (ROWS, 128), 0)
    slot48 = slot_of(row48).astype(F32)
    quarter48 = quarter_of(row48)
    row16 = jnp.where(sub16 < 8, sub16, 8 + jnp.bitwise_and(sub16, 3)).astype(F32)
    quarter_all = quarter_of(lax.broadcasted_iota(jnp.int32, (4, ROWS, 1), 1)).reshape(4 * ROWS, 1)

    def pick_rows():
        for h in range(2):
            _, own_slot = routes(h, z, y)
            for e in range(4):
                hit = own_slot[e : e + 1] == slot48
                for j in range(4):
                    d_sel[h, j, e * ROWS : (e + 1) * ROWS] = one_hot(hit & (quarter48 == j))

    def z_first(h):
        z_out[h, 0] = column_sum(h, 0).astype(BF)
        send(z_out.at[h, 0], z_opp.at[h], rz_s.at[h, 0], rz_r.at[h, 0], z_plus)

    def z_second(h):
        z_out[h, 1] = column_sum(h, 1).astype(BF)
        send(z_out.at[h, 1], z_pure.at[h], rz_s.at[h, 1], rz_r.at[h, 1], z_minus)

    def z_third(h):
        ahead = column_sum(h, 2)
        arrived(z_opp.at[h], rz_r.at[h, 0])
        z_out[h, 2] = (ahead + z_opp[h].astype(F32)).astype(BF)
        send(z_out.at[h, 2], z_rel.at[h], rz_s.at[h, 2], rz_r.at[h, 2], z_plus)

    def norm(h):
        middle = column_sum(h, 3) + res[h].astype(F32)
        arrived(z_pure.at[h], rz_r.at[h, 1])
        arrived(z_rel.at[h], rz_r.at[h, 2])
        middle = middle + z_pure[h].astype(F32) + z_rel[h].astype(F32)
        mid[h] = middle
        ss[h, 0] = jnp.broadcast_to(jnp.sum(middle * middle, axis=1, keepdims=True), (TOK, 128))
        send(ss.at[h, 0], ss.at[h, 1], ss_s.at[h], ss_r.at[h], twin)

    def slab(h, zz, yy):
        return got.at[h, c, zz, yy]

    def moe_send(h, zz, yy, number, to):
        remote(slab(h, zz, yy), slab(h, zz, yy), moe_s.at[h, number], moe_r.at[h, zz, yy], to).start()

    def moe_twin(h, zz, yy, number):
        remote(slab(h, zz, yy), slab(h, zz, yy), moe_s.at[h, number], moe_x.at[h, zz, yy], twin).start()

    def moe_wait(h, zz, yy):
        arrived(slab(h, zz, yy), moe_r.at[h, zz, yy])

    def moe_column(h, zz, number):
        moe_send(h, zz, y, number, y_plus)
        moe_send(h, zz, y, number + 1, y_minus)
        moe_twin(h, zz, y, number + 2)

    def dispatch(h):
        arrived(ss.at[h, 1], ss_r.at[h])
        scale = lax.rsqrt((ss[h, 0] + ss[h, 1])[:, 0:1] * (1.0 / D) + 1e-06)
        normed[h] = (mid[h] * scale * gain[...]).astype(BF)
        out = jnp.zeros((4 * ROWS, EIGHTH), F32)
        for j in range(4):
            cols = normed[h, :, j * EIGHTH : (j + 1) * EIGHTH]
            out = out + jnp.dot(d_sel[h, j, :, 0:TOK], cols, preferred_element_type=F32)
        disp[h] = out.astype(BF).reshape(4, ROWS, EIGHTH)
        remote(disp.at[h, zp], slab(h, z, y), moe_s.at[h, 1], moe_r.at[h, z, y], z_plus).start()
        remote(disp.at[h, zm], slab(h, z, y), moe_s.at[h, 2], moe_r.at[h, z, y], z_minus).start()
        remote(disp.at[h, zo], slab(h, z, y), moe_s.at[h, 0], moe_r.at[h, z, y], z_far).start()
        got[h, c, z, y] = disp[h, z]
        moe_column(h, z, 3)

    def moe_spread(h, zz, number):
        moe_wait(h, zz, y)
        moe_column(h, zz, number)

    def moe_behind(h, zz, i):
        moe_wait(h, zz, ym)
        moe_send(h, zz, ym, 15 + i, y_plus)
        moe_twin(h, zz, ym, 19 + i)

    def moe_ahead(h, zz, i):
        moe_wait(h, zz, yp)
        moe_twin(h, zz, yp, 23 + i)

    def moe_far(h, zz, i):
        moe_wait(h, zz, yo)
        moe_twin(h, zz, yo, 27 + i)

    def experts(h, yy, number):
        for zz in (z, zm, zp, zo):
            arrived(got.at[h, 1 - c, zz, yy], moe_x.at[h, zz, yy])
        first_rows = got[h, 0, :, yy].reshape(4 * ROWS, EIGHTH)
        second_rows = got[h, 1, :, yy].reshape(4 * ROWS, EIGHTH)
        picked = jnp.zeros((4 * ROWS, 256), F32)
        for j in range(4):
            at = j * EIGHTH
            out = jnp.dot(first_rows, w_in[at : at + EIGHTH], preferred_element_type=F32)
            out = out + jnp.dot(second_rows, w_in[HALF + at : HALF + at + EIGHTH], preferred_element_type=F32)
            picked = jnp.where(quarter_all == j, out, picked)
        for zz in range(4):
            at = zz * ROWS
            head = picked[at : at + 8] + picked[at + 8 : at + 16] + picked[at + 16 : at + 24] + picked[at + 24 : at + 32]
            tail = picked[at + 32 : at + 40] + picked[at + 40 : at + 48]
            tail = tail + pltpu.roll(tail, 4, 0)
            both = jnp.concatenate([head, tail], axis=0)
            gate, upper = both[:, 0:128], both[:, 128:256]
            shares, slot = routes(h, zz, yy)
            mine_e = sub16 == z
            share = jnp.sum(jnp.where(mine_e, shares, 0.0), axis=0, keepdims=True)
            place_e = jnp.sum(jnp.where(mine_e, slot, 0.0), axis=0, keepdims=True)
            factor = jnp.sum(jnp.where(place_e == row16, share, 0.0), axis=1, keepdims=True)
            hidden = factor * (gate * (1.0 / (1.0 + jnp.exp(-gate))) * upper)
            low, high = hidden[0:8], hidden[8:16]
            hid[h, yy, at : at + ROWS, wd_c] = jnp.concatenate([low, low, low, low, high, high], axis=0).astype(BF)
        here = hid.at[h, yy, :, wd_c]
        remote(here, here, hid_s.at[h, number], hid_r.at[h, yy], twin).start()

    def down(h, yy):
        arrived(hid.at[h, yy, :, wd_x], hid_r.at[h, yy])
        rows = hid[h, yy]
        out = jnp.zeros((4 * ROWS, EIGHTH), F32)
        for j in range(4):
            term = jnp.dot(rows, wd[:, j * EIGHTH : (j + 1) * EIGHTH], preferred_element_type=F32)
            out = jnp.where(quarter_all == j, term, out)
        dpart[h, yy] = out.astype(BF).reshape(4, ROWS, EIGHTH)

    def e_behind(h, k):
        send(dpart.at[h, ym, order[k]], e_pure.at[h, k], ey_s.at[h, 4 + k], ey_r.at[h, 4 + k], y_minus)

    def e_opposite(h, k):
        send(dpart.at[h, yo, order[k]], e_opp.at[h, k], ey_s.at[h, k], ey_r.at[h, k], y_plus)

    def e_onward(h, k):
        arrived(e_opp.at[h, k], ey_r.at[h, k])
        dpart[h, yp, order[k]] = (dpart[h, yp, order[k]].astype(F32) + e_opp[h, k].astype(F32)).astype(BF)
        send(dpart.at[h, yp, order[k]], e_rel.at[h, k], ey_s.at[h, 8 + k], ey_r.at[h, 8 + k], y_plus)

    def plane_sum(h, k):
        arrived(e_pure.at[h, k], ey_r.at[h, 4 + k])
        arrived(e_rel.at[h, k], ey_r.at[h, 8 + k])
        s = dpart[h, y, order[k]].astype(F32) + e_rel[h, k].astype(F32) + e_pure[h, k].astype(F32)
        return s.astype(BF)

    def back_first(h):
        e_out[h, 0] = plane_sum(h, 0)
        send(e_out.at[h, 0], e_got.at[h, z], ez_s.at[h, 0], ez_r.at[h, z], z_far)

    def back_second(h):
        e_out[h, 1] = plane_sum(h, 1)
        send(e_out.at[h, 1], e_got.at[h, z], ez_s.at[h, 1], ez_r.at[h, z], z_minus)

    def back_third(h):
        e_out[h, 2] = plane_sum(h, 2)
        send(e_out.at[h, 2], e_got.at[h, z], ez_s.at[h, 2], ez_r.at[h, z], z_plus)

    def combine(h):
        e_got[h, z] = plane_sum(h, 3)
        for zz in (zm, zp, zo):
            arrived(e_got.at[h, zz], ez_r.at[h, zz])
        rows = e_got[h].reshape(4 * ROWS, EIGHTH)
        for j in range(4):
            pick = d_sel[h, j, :, 0:TOK]
            moe = lax.dot_general(pick, rows, (((0,), (0,)), ((), ())), preferred_element_type=F32)
            at = j * EIGHTH
            o_stage[h, :, at : at + EIGHTH] = (mid[h, :, at : at + EIGHTH] + moe).astype(BF)

    loads[3].wait()
    lax.fori_loop(0, D // 512, split, 0)
    key_behind(z, 0)
    key_wait(zm, y)
    key_send(zm, y, 5, z_plus)
    own_column(zm, 6)
    key_ahead(z, 0)
    key_column(zp, 9)
    key_ready(first_blocks)
    attend(first_blocks, (0, 1))
    key_behind(zm, 1)
    key_far(z, 0)
    attend(first_blocks, (2, 3))
    key_column(zo, 12)
    key_behind(zp, 2)
    key_ahead(zm, 1)
    key_ahead(zp, 2)
    key_far(zm, 1)
    key_ready(second_blocks)
    attend(second_blocks, (2, 3))
    key_behind(zo, 3)
    attend(second_blocks, (0, 1))
    key_ahead(zo, 3)
    key_far(zp, 2)
    key_far(zo, 3)
    key_ready(third_blocks)
    attend(third_blocks, (0, 1))
    attend(third_blocks, (2, 3))
    key_ready(last_blocks)
    loads[1].wait()
    finish(yo, 3)
    finish(ym, 1)
    loads[2].wait()
    arrived(wo.at[1 - c], w_r.at[0])
    project(yo)
    opposite(1, 0)
    opposite(0, 2)
    opposite(1, 1)
    opposite(0, 1)
    opposite(1, 2)
    opposite(0, 0)
    pick_rows()
    finish(y, 0)
    opposite(1, 3)
    finish(yp, 2)
    project(yp)
    onward(1, 0)
    project(y)
    project(ym)
    behind(1, 0)
    behind(0, 0)
    onward(1, 2)
    onward(0, 0)
    onward(1, 1)
    behind(1, 1)
    behind(1, 2)
    behind(0, 2)
    onward(0, 2)
    behind(1, 3)
    behind(0, 1)
    onward(0, 1)
    opposite(0, 3)
    onward(1, 3)
    behind(0, 3)
    z_first(1)
    z_first(0)
    z_second(1)
    z_third(1)
    z_third(0)
    z_second(0)
    onward(0, 3)
    loads[5].wait()
    loads[6].wait()
    arrived(res.at[1 - c], w_r.at[2])
    norm(1)
    dispatch(1)
    norm(0)
    dispatch(0)
    moe_behind(1, z, 0)
    moe_ahead(1, z, 0)
    moe_spread(1, zm, 6)
    moe_spread(1, zp, 9)
    moe_behind(0, z, 0)
    moe_ahead(0, z, 0)
    moe_far(1, z, 0)
    moe_behind(1, zm, 1)
    moe_ahead(1, zm, 1)
    moe_behind(1, zp, 2)
    moe_spread(1, zo, 12)
    moe_spread(0, zm, 6)
    moe_ahead(1, zp, 2)
    moe_far(0, z, 0)
    experts(1, y, 0)
    moe_far(1, zm, 1)
    moe_spread(0, zp, 9)
    moe_far(1, zp, 2)
    loads[4].wait()
    arrived(wd.at[wd_x], w_r.at[1])
    down(1, y)
    moe_behind(1, zo, 3)
    moe_ahead(1, zo, 3)
    moe_behind(0, zm, 1)
    experts(1, yp, 2)
    moe_spread(0, zo, 12)
    moe_behind(0, zp, 2)
    experts(1, ym, 1)
    moe_far(1, zo, 3)
    experts(0, y, 0)
    experts(1, yo, 3)
    moe_behind(0, zo, 3)
    down(1, ym)
    e_behind(1, 1)
    down(1, yo)
    e_opposite(1, 1)
    e_opposite(1, 0)
    moe_ahead(0, zp, 2)
    e_opposite(1, 2)
    moe_far(0, zp, 2)
    moe_ahead(0, zo, 3)
    e_behind(1, 0)
    down(1, yp)
    moe_far(0, zm, 1)
    e_behind(1, 2)
    moe_far(0, zo, 3)
    moe_ahead(0, zm, 1)
    experts(0, yp, 2)
    e_onward(1, 1)
    experts(0, yo, 3)
    e_onward(1, 0)
    e_onward(1, 2)
    down(0, y)
    down(0, yo)
    e_opposite(0, 0)
    e_opposite(0, 1)
    e_opposite(0, 2)
    experts(0, ym, 1)
    back_second(1)
    down(0, ym)
    back_third(1)
    e_behind(0, 3)
    e_behind(0, 0)
    e_behind(0, 2)
    down(0, yp)
    e_onward(0, 0)
    e_behind(0, 1)
    e_onward(0, 1)
    e_behind(1, 3)
    back_first(1)
    e_opposite(0, 3)
    e_onward(0, 2)
    e_opposite(1, 3)
    back_first(0)
    back_second(0)
    e_onward(0, 3)
    back_third(0)
    e_onward(1, 3)
    combine(1)
    combine(0)
    send(o_stage.at[1 - c], out_ref.at[:, half_c], o_s.at[0], o_r.at[0], twin)
    out_ref[:, half_c] = o_stage[c]
    arrived(out_ref.at[:, half_x], o_r.at[0])

    for k in range(1, NSEC):
        g = (sec - k + NSEC) % NSEC
        arrived(pages_ref.at[g], page_r.at[k - 1])
    for copy in sent:
        copy.wait_send()

    def key_done(i, carry):
        remote(block(z, y), block(z, y), key_s.at[i], key_r.at[z, y], twin).wait_send()
        return carry

    lax.fori_loop(0, N_KEY, key_done, 0)

    def moe_done(i, carry):
        for h in range(2):
            remote(slab(h, z, y), slab(h, z, y), moe_s.at[h, i], moe_r.at[h, z, y], twin).wait_send()
        return carry

    lax.fori_loop(0, N_MOE, moe_done, 0)

    def hid_done(i, carry):
        for h in range(2):
            here = hid.at[h, i, :, wd_c]
            remote(here, here, hid_s.at[h, i], hid_r.at[h, i], twin).wait_send()
        return carry

    lax.fori_loop(0, 4, hid_done, 0)


def body(
    queries, stretch_latents, pool_latents, stretch_offset, value_up, out_proj, resid, norm_gain,
    expert_ids, route_weight, gate_up, down_proj, page_owner,
):
    anywhere = pl.BlockSpec(memory_space=pl.ANY)
    vmem = pl.BlockSpec(memory_space=pltpu.VMEM)
    smem = pl.BlockSpec(memory_space=pltpu.SMEM)
    V = pltpu.VMEM
    S = lambda *shape: pltpu.SemaphoreType.DMA(shape)
    scratch = [
        V((STRETCH, 2 * LATW), BF), V((4, TILE, WIDE), BF), V((4, 4, 2 * BLK, WIDE), BF),
        V((4, TILE, LAT), F32), V((4, TILE, 128), F32), V((4, TILE, 128), F32),
        V((2, 4, 128, 256), BF), V((2, 256, HALF), BF), V((256, HALF), BF),
        V((2 * D, 128), BF), V((D, 256), BF), V((2, LAT, HEAD_DIM), BF),
        V((2, TOK, HALF), BF), V((1, HALF), F32),
        V((NSEC, TOK, LATW), BF), V((4, 4, 32, HALF), BF),
        V((2, 4, TOK, HALF), BF), V((2, 4, TOK, HALF), BF), V((2, 4, TOK, HALF), BF),
        V((2, 3, TOK, HALF), BF), V((2, TOK, HALF), BF), V((2, TOK, HALF), BF), V((2, TOK, HALF), BF),
        V((2, TOK, HALF), F32), V((2, TOK, HALF), BF), V((2, 2, TOK, 128), F32),
        V((2, 4, 4 * ROWS, 128), BF),
        V((2, 4, ROWS, EIGHTH), BF), V((2, 2, 4, 4, ROWS, EIGHTH), BF),
        V((2, 4, 4 * ROWS, 256), BF),
        V((2, 4, 4, ROWS, EIGHTH), BF),
        V((2, 4, ROWS, EIGHTH), BF), V((2, 4, ROWS, EIGHTH), BF), V((2, 4, ROWS, EIGHTH), BF),
        V((2, 3, ROWS, EIGHTH), BF), V((2, 4, ROWS, EIGHTH), BF),
        V((2, TOK, HALF), BF),
        S(7), S(N_KEY), S(4, 4), S(4, 4), S(3), S(3), S(4), S(4), S(7), S(7),
        S(2, 12), S(2, 12), S(2, 3), S(2, 3), S(2), S(2),
        S(2, N_MOE), S(2, 4, 4), S(2, 4, 4), S(2, 4), S(2, 4),
        S(2, 12), S(2, 12), S(2, 3), S(2, 4), S(1), S(1),
    ]
    out, pages = pl.pallas_call(
        kernel,
        out_shape=(
            jax.ShapeDtypeStruct((TOK, D), BF),
            jax.ShapeDtypeStruct((NSEC, TOK, LATW), BF),
        ),
        in_specs=[smem, smem, anywhere, vmem, vmem, anywhere, anywhere, anywhere, anywhere, vmem, vmem, anywhere, anywhere],
        out_specs=(vmem, vmem),
        scratch_shapes=scratch,
        compiler_params=pltpu.CompilerParams(
            collective_id=0, has_side_effects=True, vmem_limit_bytes=60 * 1024 * 1024
        ),
    )(
        stretch_offset,
        page_owner[0],
        queries[0],
        stretch_latents[0],
        pool_latents[0],
        value_up[0],
        out_proj[0],
        resid[0],
        norm_gain,
        expert_ids[0].T,
        route_weight[0].T,
        gate_up[0, 0].reshape(2 * D, 128),
        down_proj[0, 0],
    )
    return out[None], pages.reshape(1, 1, NSEC, TOK * LATW)


def solution(mesh):
    placed = (
        P("section", None, "expert"),
        P("section", "expert", None),
        P("section", "expert", None),
        P("section"),
        P("section", "expert", None, None),
        P("section", "expert", None),
        P("section", "expert", None),
        P("section", None),
        P("section", "expert", None),
        P("section", "expert", None),
        P("section", "expert", None, None, None),
        P("section", "expert", None, None),
        P("section", "expert"),
    )
    return jax.shard_map(
        body,
        mesh=mesh,
        in_specs=placed,
        out_specs=(P("section", "expert", None), P("section", "expert", None, None)),
        check_vma=False,
    )
```
